32 devices in a mesh: img: 8 (over y, x, core), blk: 4 (over z).
Axes of the slice: x: 2, y: 2, z: 4, core: 2. Of those that a mesh axis runs over, the one named last changes fastest.
Arguments:
- images: bfloat16 [32, 28, 1792], P('img'), may hold values from -6 to 6
- filters: bfloat16 [2048, 576], P('blk'), may hold values from -0.5 to 0.5
- phases: float32 [2048], P('blk'), may hold values from -3.140625 to 3.140625
- labels: int32 [6272], P('img'), may hold values from 0 to 149
- weights: float32 [150, 2048], P(None, 'blk'), may hold values from -6 to 6
Outputs:
- new_weights: float32 [150, 2048], P(None, 'blk')
- residual: float32 [150, 6272], P(None, 'img')
The draws below stay inside these ranges and needn't reach their ends.
All inputs are finite; a program needn't handle non-finite values.
Results may differ from the reference program's by a relative error of at most 0.015.
Values may be sent and summed in bfloat16 or wider, within the bound.
A program may use at most 64 MiB of HBM per device.

```python
import math
import jax
import jax.numpy as jnp
from jax import lax

SIDE = 28
CHAN = 64
FILT = 512
LABELS = 150
ITERS = 2
IMAGES = 32
PIXELS = 6272
FEATURES = 2048


def draw_filters(key, part):
    key_values = jax.random.fold_in(key, 11)
    tap_count = 9 * CHAN
    values = jax.random.normal(key_values, (FEATURES, tap_count), jnp.float32)
    return jnp.clip(values / math.sqrt(tap_count), -0.5, 0.5).astype(jnp.bfloat16)


def set_ends(array, key, smallest, high):
    longest = array.shape.index(max(array.shape))
    spots = []
    for shift in (0, 1):
        where = [jax.random.randint(jax.random.fold_in(key, axis), (), 0, length) for axis, length in enumerate(array.shape)]
        where[longest] = (where[longest] + shift) % array.shape[longest]
        spots.append(tuple(where))
    return array.at[spots[0]].set(smallest).at[spots[1]].set(high)


def levels(own_key, shape, split, low, largest):
    def one(axis_at, shards_of):
        draws = jax.random.uniform(jax.random.fold_in(jax.random.fold_in(own_key, 6), axis_at), (shards_of,), jnp.float32, low / len(split), largest / len(split))
        return jnp.repeat(jnp.exp(draws), shape[axis_at] // shards_of).reshape((-1,) + (1,) * (len(shape) - axis_at - 1))

    gain = one(*split[0])
    for cut in split[1:]:
        gain = gain * one(*cut)
    return gain


def noise(stream_key, dims, scale, reach, shards=(), kind=jnp.bfloat16):
    entries = scale * jax.random.normal(stream_key, dims, jnp.float32)
    if shards:
        entries = entries * levels(stream_key, dims, shards, -0.22, 0.18)
    return jnp.clip(entries, -reach, reach).astype(kind)


def setup_inputs(seed: int = 0) -> dict:
    streams_of = jax.random.split(jax.random.key(seed), 6)
    return {
        "images": noise(streams_of[0], (IMAGES, SIDE, SIDE * CHAN), 1.0, 6.0, ((0, 8),)),
        "filters": draw_filters(jax.random.fold_in(streams_of[5], 71), 0),
        "phases": jnp.clip(jax.random.uniform(streams_of[2], (FEATURES,), jnp.float32, -3.140625, 3.140625), -3.140625, 3.140625),
        "labels": set_ends(jax.random.randint(streams_of[3], (PIXELS,), 0, LABELS), jax.random.fold_in(streams_of[3], 1), 0, LABELS - 1).astype(jnp.int32),
        "weights": noise(streams_of[4], (LABELS, FEATURES), 1.0, 6.0, ((1, 4),), jnp.float32),
    }


RIDGE = 0.5
DAMPING = 0.75

def block_features(images, filter_rows, phase_rows):
    count_images = images.shape[0]
    pictures = images.reshape(count_images, SIDE, SIDE, CHAN)
    kernel = filter_rows.reshape(filter_rows.shape[0], 3, 3, CHAN)
    response = lax.conv_general_dilated(pictures, kernel, (2, 2), ((1, 1), (1, 1)), dimension_numbers=('NHWC', 'OHWI', 'CNHW'), preferred_element_type=jnp.float32)
    response = response.reshape(filter_rows.shape[0], count_images * (SIDE // 2) ** 2)
    return (math.sqrt(2.0) * jnp.cos(response + phase_rows[:, None])).astype(jnp.bfloat16)

def solve_with(factor, projected):
    middle = lax.linalg.triangular_solve(factor, projected, left_side=False, lower=True, transpose_a=True)
    return lax.linalg.triangular_solve(factor, middle, left_side=False, lower=True, transpose_a=False)

def reference(images, filters, phases, labels, weights):
    blocks = filters.shape[0] // FILT
    features_all = FILT * blocks
    shrink = 1.0 / math.sqrt(features_all)
    expand = math.sqrt(features_all)
    pixels = labels.shape[0]
    targets = (labels[None, :] == jnp.arange(LABELS, dtype=jnp.int32)[:, None]).astype(jnp.float32)
    filter_blocks = filters.reshape(blocks, FILT, filters.shape[1])
    phase_blocks = phases.reshape(blocks, FILT)
    weight_blocks = weights.reshape(LABELS, blocks, FILT).transpose(1, 0, 2)
    identity = jnp.eye(FILT, dtype=jnp.float32)

    def first_pass(summed, inputs):
        filter_rows, phase_rows, weight_now = inputs
        features = block_features(images, filter_rows, phase_rows)
        gram = lax.dot_general(features.astype(jnp.float32), features.astype(jnp.float32), (((1,), (1,)), ((), ())), preferred_element_type=jnp.float32) + RIDGE * pixels * identity
        factor = jnp.linalg.cholesky(gram)
        partial_value = (shrink * jnp.dot(weight_now.astype(jnp.bfloat16).astype(jnp.float32), features.astype(jnp.float32), preferred_element_type=jnp.float32)).astype(jnp.bfloat16)
        return (summed + partial_value, factor)
    zeros_start = jnp.zeros((LABELS, pixels), jnp.float32)
    predicted, factors = lax.scan(first_pass, zeros_start, (filter_blocks, phase_blocks, weight_blocks))
    residual = targets - predicted
    for step in range(ITERS):
        residual_half = residual.astype(jnp.bfloat16)

        def update_pass(summed, inputs):
            filter_rows, phase_rows, weight_now, factor = inputs
            features = block_features(images, filter_rows, phase_rows)
            projected = lax.dot_general(residual_half.astype(jnp.float32), features.astype(jnp.float32), (((1,), (1,)), ((), ())), preferred_element_type=jnp.float32)
            change = expand * solve_with(factor, projected)
            weight_next = weight_now + DAMPING * change
            partial_value = (shrink * jnp.dot(weight_next.astype(jnp.bfloat16).astype(jnp.float32), features.astype(jnp.float32), preferred_element_type=jnp.float32)).astype(jnp.bfloat16)
            return (summed + partial_value, weight_next)
        predicted, weight_blocks = lax.scan(update_pass, zeros_start, (filter_blocks, phase_blocks, weight_blocks, factors))
        residual = targets - predicted
    new_weights = weight_blocks.transpose(1, 0, 2).reshape(LABELS, features_all)
    return (new_weights, residual)
```

```python
import math

import jax
import jax.numpy as jnp
import numpy as np
from jax import lax
from jax.experimental import pallas as pl
from jax.experimental.pallas import tpu as pltpu
from jax.sharding import PartitionSpec as P

SIDE = 28
CHAN = 64
LABELS = 150
ITERS = 2
RIDGE = 0.5
DAMPING = 0.75
TILE = 128


def cosine_coefficients(degree=6):
    nodes = np.cos((np.arange(400) + 0.5) * np.pi / 400)
    square = (nodes + 1.0) * (np.pi**2 * 1.0005) / 2
    fit = np.polynomial.chebyshev.Chebyshev.fit(square, np.sqrt(2.0) * np.cos(np.sqrt(square)), degree)
    return [float(c) for c in fit.convert(kind=np.polynomial.Polynomial).coef]


COEFFICIENTS = cosine_coefficients()
TURN_HIGH = 6.28125
TURN_LOW = 2.0 * math.pi - TURN_HIGH


def inverse_scales(lowest):
    scales = []
    while 1.0 - lowest > 1e-6:
        scale = 2.0 / (1.0 + lowest)
        scales.append(scale)
        lowest = scale * lowest * (2.0 - scale * lowest)
    return scales


def split(value):
    high = value.astype(jnp.bfloat16)
    return high, (value - high.astype(jnp.float32)).astype(jnp.bfloat16)


def dot(a, b):
    return jnp.dot(a, b, preferred_element_type=jnp.float32)


def dot_nt(a, b):
    return lax.dot_general(a, b, (((1,), (1,)), ((), ())), preferred_element_type=jnp.float32)


def dot_three(a_high, a_low, b_high, b_low):
    return dot(a_high, b_high) + (dot(a_high, b_low) + dot(a_low, b_high))


def make_kernel(n_img, n_blk, filt, pos, pos_pad, pixels, rows_img, rows_blk, rows_all):
    features_all = filt * n_blk
    shrink = 1.0 / math.sqrt(features_all)
    expand = math.sqrt(features_all)
    tiles = filt // TILE
    packed = tiles * (tiles + 1) // 2 * TILE
    rows_gram = packed // n_img
    upper = (RIDGE + 2.0 * filt) * pixels
    scales = inverse_scales(RIDGE * pixels / upper)

    def kernel(
        patches_ref, filters_ref, phases_ref, labels_ref, weights_ref, scales_ref,
        out_weights, out_residual,
        feat, gram, gram_in, gram_all, h_high, h_low, x_now, x_high, x_low, y_high, y_low,
        part, part_in, part_all, resid, proj, proj_in, w_own, w_all,
        gram_s, gram_r, gram_all_s, gram_all_r,
        part_s, part_r, part_all_s, part_all_r,
        proj_s, proj_r, w_s, w_r,
    ):
        img = lax.axis_index("img")
        blk = lax.axis_index("blk")
        barrier = pltpu.get_barrier_semaphore()

        def each_peer(me, n, body):
            def one(step, carry):
                body(step, lax.rem(me + step, n))
                return carry

            lax.fori_loop(1, n, one, 0)

        each_peer(img, n_img, lambda step, peer: pl.semaphore_signal(
            barrier, inc=1, device_id={"img": peer}, device_id_type=pl.DeviceIdType.MESH))
        each_peer(blk, n_blk, lambda step, peer: pl.semaphore_signal(
            barrier, inc=1, device_id={"blk": peer}, device_id_type=pl.DeviceIdType.MESH))

        def scatter(axis, me, n, rows, source, target, send, recv):
            def copy(step, peer, slot):
                return pltpu.make_async_remote_copy(
                    src_ref=source.at[pl.ds(pl.multiple_of(peer * rows, 8), rows)],
                    dst_ref=target.at[slot],
                    send_sem=send.at[step], recv_sem=recv.at[slot],
                    device_id={axis: peer}, device_id_type=pl.DeviceIdType.MESH)

            def start():
                each_peer(me, n, lambda step, peer: copy(step, peer, me).start())
                target[me] = source[pl.ds(pl.multiple_of(me * rows, 8), rows), :]

            def wait():
                each_peer(me, n, lambda step, peer: copy(step, peer, peer).wait_recv())

            def wait_sent():
                each_peer(me, n, lambda step, peer: copy(step, peer, me).wait_send())

            return start, wait, wait_sent

        def gather(axis, me, n, rows, whole, send, recv):
            def copy(step, peer, slot):
                place = whole.at[pl.ds(pl.multiple_of(slot * rows, 8), rows)]
                return pltpu.make_async_remote_copy(
                    src_ref=place, dst_ref=place,
                    send_sem=send.at[step], recv_sem=recv.at[slot],
                    device_id={axis: peer}, device_id_type=pl.DeviceIdType.MESH)

            def start(value):
                whole[pl.ds(pl.multiple_of(me * rows, 8), rows), :] = value
                each_peer(me, n, lambda step, peer: copy(step, peer, me).start())

            def wait():
                each_peer(me, n, lambda step, peer: copy(step, peer, peer).wait_recv())

            def wait_sent():
                each_peer(me, n, lambda step, peer: copy(step, peer, me).wait_send())

            return start, wait, wait_sent

        unsent = []

        inside = lax.broadcasted_iota(jnp.int32, (TILE, pos_pad), 1) < pos
        for tile in range(tiles):
            here = slice(tile * TILE, (tile + 1) * TILE)
            angle = dot_nt(filters_ref[here, :], patches_ref[...]) + phases_ref[here, :]
            turns = jnp.floor(angle * (0.5 / math.pi) + 0.5)
            angle = (angle - turns * TURN_HIGH) - turns * TURN_LOW
            square = angle * angle
            value = jnp.full_like(square, COEFFICIENTS[-1])
            for coefficient in COEFFICIENTS[-2::-1]:
                value = value * square + coefficient
            feat[here, :] = jnp.where(inside, value, 0.0).astype(jnp.bfloat16)

        spot = 0
        for row in range(tiles):
            block = dot_nt(feat[row * TILE:(row + 1) * TILE, :], feat[: (row + 1) * TILE, :])
            for col in range(row + 1):
                gram[spot * TILE:(spot + 1) * TILE, :] = block[:, col * TILE:(col + 1) * TILE]
                spot += 1

        pl.semaphore_wait(barrier, n_img - 1 + n_blk - 1)
        gram_scatter = scatter("img", img, n_img, rows_gram, gram, gram_in, gram_s, gram_r)
        gram_gather = gather("img", img, n_img, rows_gram, gram_all, gram_all_s, gram_all_r)
        gram_scatter[0]()

        def begin_predict(turn, weight_now):
            send = scatter("blk", blk, n_blk, rows_blk, part.at[turn], part_in.at[turn],
                           part_s.at[turn], part_r.at[turn])
            part[turn] = (shrink * dot(weight_now, feat[...])).astype(jnp.bfloat16)
            send[0]()
            return send

        def middle_predict(turn, send):
            share = gather("blk", blk, n_blk, rows_blk, part_all.at[turn],
                           part_all_s.at[turn], part_all_r.at[turn])
            send[1]()
            total = jnp.sum(part_in[turn].astype(jnp.float32), axis=0)
            share[0](total.astype(jnp.bfloat16))
            unsent.extend([send[2], share[2]])
            return share

        def end_predict(turn, share):
            share[1]()
            classes = lax.broadcasted_iota(jnp.int32, (rows_all, pos_pad), 0)
            targets = jnp.where(labels_ref[...] == classes, 1.0, 0.0)
            return targets - part_all[turn].astype(jnp.float32)

        def begin_project(step):
            send = scatter("img", img, n_img, rows_img, proj.at[step], proj_in.at[step],
                           proj_s.at[step], proj_r.at[step])
            proj[step] = dot_nt(resid[...], feat[...])
            send[0]()
            return send

        def solve_step(step, send):
            send[1]()
            p_high, p_low = split(jnp.sum(proj_in[step], axis=0))
            change = expand * dot_three(p_high, p_low, x_high[...], x_low[...])
            w_own[...] += DAMPING * change
            share = gather("img", img, n_img, rows_img, w_all.at[step], w_s.at[step], w_r.at[step])
            share[0](w_own[...])
            share[1]()
            unsent.extend([send[2], share[2]])

        predict_send = begin_predict(0, weights_ref[...].astype(jnp.bfloat16))
        w_own[...] = weights_ref[pl.ds(pl.multiple_of(img * rows_img, 8), rows_img), :]
        if rows_all > n_img * rows_img:
            for step in range(ITERS):
                w_all[step] = jnp.zeros((rows_all, filt), jnp.float32)

        gram_scatter[1]()
        gram_gather[0](jnp.sum(gram_in[...], axis=0))
        unsent.extend([gram_scatter[2], gram_gather[2]])
        share = middle_predict(0, predict_send)
        gram_gather[1]()

        spot = 0
        diagonal = (lax.broadcasted_iota(jnp.int32, (TILE, TILE), 0)
                    == lax.broadcasted_iota(jnp.int32, (TILE, TILE), 1))
        first = scales[0]
        for row in range(tiles):
            for col in range(row + 1):
                block = gram_all[spot * TILE:(spot + 1) * TILE, :]
                spot += 1
                if row == col:
                    block = block + jnp.where(diagonal, RIDGE * pixels, 0.0)
                start = block * (-first * first / upper / upper)
                if row == col:
                    start = start + jnp.where(diagonal, 2.0 * first / upper, 0.0)
                places = [(row, col, block, start)]
                if row != col:
                    places.append((col, row, block.T, start.T))
                for down, across, h_part, x_part in places:
                    at = (slice(down * TILE, (down + 1) * TILE), slice(across * TILE, (across + 1) * TILE))
                    h_high[at], h_low[at] = split(h_part)
                    x_now[at] = x_part
                    x_high[at], x_low[at] = split(x_part)

        resid[...] = end_predict(0, share).astype(jnp.bfloat16)
        project_send = begin_project(0)

        def newton(step, carry):
            scale = scales_ref[step]
            y = dot_three(h_high[...], h_low[...], x_high[...], x_low[...]) * (-scale)
            same = (lax.broadcasted_iota(jnp.int32, (filt, filt), 0)
                    == lax.broadcasted_iota(jnp.int32, (filt, filt), 1))
            y_high[...], y_low[...] = split(y + jnp.where(same, 2.0, 0.0))
            x = dot_three(x_high[...], x_low[...], y_high[...], y_low[...]) * scale
            x_high[...], x_low[...] = split(x)
            return carry

        lax.fori_loop(1, len(scales), newton, 0)

        for step in range(ITERS):
            solve_step(step, project_send)
            send = begin_predict(step + 1, w_all[step].astype(jnp.bfloat16))
            if step == ITERS - 1:
                out_weights[...] = w_all[step, :LABELS, :]
            share = middle_predict(step + 1, send)
            residual = end_predict(step + 1, share)
            if step < ITERS - 1:
                resid[...] = residual.astype(jnp.bfloat16)
                project_send = begin_project(step + 1)
            else:
                out_residual[...] = residual[:LABELS, :pos]
        for wait_sent in unsent:
            wait_sent()

    f32, bf16 = jnp.float32, jnp.bfloat16
    square = (filt, filt)
    dma = pltpu.SemaphoreType.DMA
    turns = ITERS + 1
    scratch = [
        pltpu.VMEM((filt, pos_pad), bf16),
        pltpu.VMEM((packed, TILE), f32),
        pltpu.VMEM((n_img, rows_gram, TILE), f32),
        pltpu.VMEM((packed, TILE), f32),
        pltpu.VMEM(square, bf16), pltpu.VMEM(square, bf16),
        pltpu.VMEM(square, f32), pltpu.VMEM(square, bf16), pltpu.VMEM(square, bf16),
        pltpu.VMEM(square, bf16), pltpu.VMEM(square, bf16),
        pltpu.VMEM((turns, rows_all, pos_pad), bf16),
        pltpu.VMEM((turns, n_blk, rows_blk, pos_pad), bf16),
        pltpu.VMEM((turns, rows_all, pos_pad), bf16),
        pltpu.VMEM((rows_all, pos_pad), bf16),
        pltpu.VMEM((ITERS, rows_all, filt), f32),
        pltpu.VMEM((ITERS, n_img, rows_img, filt), f32),
        pltpu.VMEM((rows_img, filt), f32),
        pltpu.VMEM((ITERS, rows_all, filt), f32),
        dma((n_img,)), dma((n_img,)), dma((n_img,)), dma((n_img,)),
        dma((turns, n_blk)), dma((turns, n_blk)), dma((turns, n_blk)), dma((turns, n_blk)),
        dma((ITERS, n_img)), dma((ITERS, n_img)), dma((ITERS, n_img)), dma((ITERS, n_img)),
    ]
    return kernel, scratch, scales


def round_up(value, unit):
    return -(-value // unit) * unit


def make_patches(images, pos_pad):
    count = images.shape[0]
    half = SIDE // 2
    pairs = images.reshape(count, SIDE, half, 2 * CHAN)
    pairs = jnp.pad(pairs, ((0, 0), (1, 1), (1, 0), (0, 0)))
    parts = []
    for row in range(3):
        lines = pairs[:, row:row + SIDE:2]
        parts += [lines[:, :, :half], lines[:, :, 1:]]
    patches = jnp.concatenate(parts, axis=-1).reshape(count * half * half, 12 * CHAN)
    return jnp.pad(patches, ((0, pos_pad - patches.shape[0]), (0, 0)))


def solution(mesh):
    n_img, n_blk = mesh.shape["img"], mesh.shape["blk"]

    def shards(images, filters, phases, labels, weights):
        filt, pos = filters.shape[0], labels.shape[0]
        pos_pad = round_up(pos, TILE)
        rows_img = round_up(LABELS, 8 * n_img) // n_img
        rows_blk = round_up(LABELS, 16 * n_blk) // n_blk
        rows_all = max(rows_img * n_img, rows_blk * n_blk)
        kernel, scratch, scales = make_kernel(
            n_img, n_blk, filt, pos, pos_pad, pos * n_img, rows_img, rows_blk, rows_all)
        patches = make_patches(images, pos_pad)
        taps = jnp.pad(filters.reshape(filt, 3, 3 * CHAN), ((0, 0), (0, 0), (CHAN, 0)))
        vmem = pl.BlockSpec(memory_space=pltpu.VMEM)
        return pl.pallas_call(
            kernel,
            out_shape=(jax.ShapeDtypeStruct((LABELS, filt), jnp.float32),
                       jax.ShapeDtypeStruct((LABELS, pos), jnp.float32)),
            in_specs=[vmem] * 5 + [pl.BlockSpec(memory_space=pltpu.SMEM)],
            out_specs=(vmem, vmem),
            scratch_shapes=scratch,
            compiler_params=pltpu.CompilerParams(
                collective_id=0, has_side_effects=True, vmem_limit_bytes=48 * 2**20),
        )(
            patches,
            taps.reshape(filt, 12 * CHAN),
            phases[:, None],
            jnp.pad(labels[None, :], ((0, 0), (0, pos_pad - pos)), constant_values=-1),
            jnp.pad(weights, ((0, rows_all - LABELS), (0, 0))),
            jnp.asarray(np.array(scales, np.float32)),
        )

    return jax.shard_map(
        shards,
        mesh=mesh,
        in_specs=(P("img", None, None), P("blk", None), P("blk"), P("img"), P(None, "blk")),
        out_specs=(P(None, "blk"), P(None, "img")),
        check_vma=False,
    )
```

```python
import math

import jax
import jax.numpy as jnp
import numpy as np
from jax import lax
from jax.experimental import pallas as pl
from jax.experimental.pallas import tpu as pltpu
from jax.sharding import PartitionSpec as P

SIDE = 28
CHAN = 64
LABELS = 150
ITERS = 2
RIDGE = 0.5
DAMPING = 0.75
TILE = 128


def cosine_coefficients(degree=6):
    nodes = np.cos((np.arange(400) + 0.5) * np.pi / 400)
    square = (nodes + 1.0) * (np.pi**2 * 1.0005) / 2
    fit = np.polynomial.chebyshev.Chebyshev.fit(square, np.sqrt(2.0) * np.cos(np.sqrt(square)), degree)
    return [float(c) for c in fit.convert(kind=np.polynomial.Polynomial).coef]


COEFFICIENTS = cosine_coefficients()
TURN_HIGH = 6.28125
TURN_LOW = 2.0 * math.pi - TURN_HIGH


def inverse_scales(lowest):
    scales = []
    while 1.0 - lowest > 1e-4:
        scale = 2.0 / (1.0 + lowest)
        scales.append(scale)
        lowest = scale * lowest * (2.0 - scale * lowest)
    return scales


def split(value):
    high = value.astype(jnp.bfloat16)
    return high, (value - high.astype(jnp.float32)).astype(jnp.bfloat16)


def dot(a, b):
    return jnp.dot(a, b, preferred_element_type=jnp.float32)


def dot_nt(a, b):
    return lax.dot_general(a, b, (((1,), (1,)), ((), ())), preferred_element_type=jnp.float32)


def dot_three(a_high, a_low, b_high, b_low):
    return dot(a_high, b_high) + (dot(a_high, b_low) + dot(a_low, b_high))


def make_groups(n_img, n_blk):
    unit = math.lcm(8 * n_img, 16 * n_blk)
    chunks = {"img": unit // n_img, "blk": unit // n_blk}
    last = math.lcm(*chunks.values())
    groups = []
    first = 0
    while first < LABELS:
        rows = min(unit, round_up(LABELS - first, last))
        groups.append((first, rows))
        first += rows
    return groups, chunks


def make_kernel(n_img, n_blk, filt, pos, pos_pad, pixels, groups, chunks):
    features_all = filt * n_blk
    shrink = 1.0 / math.sqrt(features_all)
    expand = math.sqrt(features_all)
    tiles = filt // TILE
    packed = tiles * (tiles + 1) // 2 * TILE
    rows_gram = packed // n_img
    rows_all = sum(rows for _, rows in groups)
    upper = (RIDGE + 2.0 * filt) * pixels
    scales = inverse_scales(RIDGE * pixels / upper)

    def kernel(
        patches_ref, filters_ref, phases_ref, labels_ref, weights_ref, scales_ref,
        out_weights, out_residual,
        feat, gram, gram_in, gram_all, h_high, h_low, x_high, x_low, y_high, y_low,
        part, part_in, part_all, proj, proj_in, w_all,
        gram_s, gram_r, gram_all_s, gram_all_r,
        part_s, part_r, part_all_s, part_all_r,
        proj_s, proj_r, w_s, w_r,
    ):
        place = {"img": lax.axis_index("img"), "blk": lax.axis_index("blk")}
        size = {"img": n_img, "blk": n_blk}
        barrier = pltpu.get_barrier_semaphore()

        def each_peer(axis, body, owners=None):
            me, n = place[axis], size[axis]
            stride = 1 if owners is None else n // owners

            def one(step, carry):
                peer = lax.rem(me + step, n)
                if owners is None or owners == n:
                    body(step, peer, peer)
                else:
                    @pl.when((lax.rem(peer, stride) == 0) & (peer < stride * owners))
                    def _():
                        body(step, peer, peer // stride)
                return carry

            lax.fori_loop(1, n, one, 0)

        def if_owner(axis, owners, body):
            me, n = place[axis], size[axis]
            stride = n // owners
            if owners == n:
                body(me)
            else:
                @pl.when((lax.rem(me, stride) == 0) & (me < stride * owners))
                def _():
                    body(me // stride)

        for axis in size:
            each_peer(axis, lambda step, peer, owner: pl.semaphore_signal(
                barrier, inc=1, device_id={axis: peer}, device_id_type=pl.DeviceIdType.MESH))

        unsent = []

        def span(first, owner, rows):
            return pl.ds(pl.multiple_of(first + owner * rows, 8), rows)

        def scatter(axis, first, rows, owners, source, target, send, recv):
            def copy(step, peer, owner, slot):
                return pltpu.make_async_remote_copy(
                    src_ref=source.at[span(first, owner, rows)],
                    dst_ref=target.at[slot],
                    send_sem=send.at[step], recv_sem=recv.at[slot],
                    device_id={axis: peer}, device_id_type=pl.DeviceIdType.MESH)

            def start():
                me = place[axis]
                each_peer(axis, lambda step, peer, owner: copy(step, peer, owner, me).start(), owners)

                def keep(owner):
                    target[me] = source[span(first, owner, rows), :]

                if_owner(axis, owners, keep)
                unsent.append(lambda: each_peer(
                    axis, lambda step, peer, owner: copy(step, peer, owner, me).wait_send(), owners))

            def wait():
                each_peer(axis, lambda step, peer, owner: copy(step, peer, 0, peer).wait_recv())

            return start, wait

        def gather(axis, first, rows, owners, whole, send, recv):
            def copy(step, peer, owner):
                at = whole.at[span(first, owner, rows)]
                return pltpu.make_async_remote_copy(
                    src_ref=at, dst_ref=at,
                    send_sem=send.at[step], recv_sem=recv.at[owner],
                    device_id={axis: peer}, device_id_type=pl.DeviceIdType.MESH)

            def start(value):
                def share(mine):
                    whole[span(first, mine, rows), :] = value(mine)
                    each_peer(axis, lambda step, peer, owner: copy(step, peer, mine).start())

                if_owner(axis, owners, share)
                unsent.append(lambda: if_owner(axis, owners, lambda mine: each_peer(
                    axis, lambda step, peer, owner: copy(step, peer, mine).wait_send())))

            def wait():
                each_peer(axis, lambda step, peer, owner: copy(step, peer, owner).wait_recv(), owners)

            return start, wait

        inside = lax.broadcasted_iota(jnp.int32, (TILE, pos_pad), 1) < pos
        for tile in range(tiles):
            here = slice(tile * TILE, (tile + 1) * TILE)
            angle = dot_nt(filters_ref[here, :], patches_ref[...]) + phases_ref[here, :]
            turns = jnp.floor(angle * (0.5 / math.pi) + 0.5)
            angle = (angle - turns * TURN_HIGH) - turns * TURN_LOW
            square = angle * angle
            value = jnp.full_like(square, COEFFICIENTS[-1])
            for coefficient in COEFFICIENTS[-2::-1]:
                value = value * square + coefficient
            feat[here, :] = jnp.where(inside, value, 0.0).astype(jnp.bfloat16)

        spot = 0
        for row in range(tiles):
            block = dot_nt(feat[row * TILE:(row + 1) * TILE, :], feat[: (row + 1) * TILE, :])
            for col in range(row + 1):
                gram[spot * TILE:(spot + 1) * TILE, :] = block[:, col * TILE:(col + 1) * TILE]
                spot += 1

        pl.semaphore_wait(barrier, n_img - 1 + n_blk - 1)
        gram_scatter = scatter("img", 0, rows_gram, n_img, gram, gram_in, gram_s, gram_r)
        gram_gather = gather("img", 0, rows_gram, n_img, gram_all, gram_all_s, gram_all_r)
        gram_scatter[0]()

        def transfers(axis, turn, g, source, target, whole, sems):
            first, rows = groups[g]
            chunk = chunks[axis]
            at = (turn, g)
            return (scatter(axis, first, chunk, rows // chunk, source.at[turn], target.at[at],
                            sems[0].at[at], sems[1].at[at])
                    + gather(axis, first, chunk, rows // chunk, whole.at[turn],
                             sems[2].at[at], sems[3].at[at]))

        def predict_transfers(turn, g):
            return transfers("blk", turn, g, part, part_in, part_all,
                             (part_s, part_r, part_all_s, part_all_r))

        def project_transfers(step, g):
            return transfers("img", step, g, proj, proj_in, w_all, (proj_s, proj_r, w_s, w_r))

        def rows_of(g):
            first, rows = groups[g]
            return slice(first, first + rows)

        def begin_predict(turn, g, weight_now):
            value = shrink * dot(weight_now.astype(jnp.bfloat16), feat[...])
            part[turn, rows_of(g), :] = value.astype(jnp.bfloat16)
            predict_transfers(turn, g)[0]()

        def middle_predict(turn, g):
            _, wait, share, _ = predict_transfers(turn, g)
            if_owner("blk", groups[g][1] // chunks["blk"], lambda mine: wait())
            share(lambda mine: jnp.sum(part_in[turn, g].astype(jnp.float32), axis=0).astype(jnp.bfloat16))

        def end_predict(turn, g):
            predict_transfers(turn, g)[3]()
            first, rows = groups[g]
            classes = lax.broadcasted_iota(jnp.int32, (rows, pos_pad), 0) + first
            targets = jnp.where(labels_ref[...] == classes, 1.0, 0.0)
            residual = targets - part_all[turn, rows_of(g), :].astype(jnp.float32)
            if turn < ITERS:
                proj[turn, rows_of(g), :] = dot_nt(residual.astype(jnp.bfloat16), feat[...])
                project_transfers(turn, g)[0]()
            else:
                end = min(first + rows, LABELS)
                out_residual[first:end, :] = residual[:end - first, :pos]

        def solve(step, g):
            _, wait, share, _ = project_transfers(step, g)

            def weight_next(mine):
                here = span(groups[g][0], mine, chunks["img"])
                before = weights_ref[here, :] if step == 0 else w_all[step - 1, here, :]
                p_high, p_low = split(jnp.sum(proj_in[step, g], axis=0))
                change = expand * dot_three(p_high, p_low, x_high[...], x_low[...])
                return before + DAMPING * change

            if_owner("img", groups[g][1] // chunks["img"], lambda mine: wait())
            share(weight_next)

        def use_weights(step, g):
            project_transfers(step, g)[3]()
            begin_predict(step + 1, g, w_all[step, rows_of(g), :])
            if step == ITERS - 1:
                first, rows = groups[g]
                end = min(first + rows, LABELS)
                out_weights[first:end, :] = w_all[step, first:end, :]

        every = range(len(groups))
        for g in every:
            begin_predict(0, g, weights_ref[rows_of(g), :])
        gram_scatter[1]()
        gram_gather[0](lambda mine: jnp.sum(gram_in[...], axis=0))
        for g in every:
            middle_predict(0, g)
        gram_gather[1]()

        spot = 0
        diagonal = (lax.broadcasted_iota(jnp.int32, (TILE, TILE), 0)
                    == lax.broadcasted_iota(jnp.int32, (TILE, TILE), 1))
        scale = scales[0]
        for row in range(tiles):
            for col in range(row + 1):
                block = gram_all[spot * TILE:(spot + 1) * TILE, :]
                spot += 1
                if row == col:
                    block = block + jnp.where(diagonal, RIDGE * pixels, 0.0)
                start = block * (-scale * scale / upper / upper)
                if row == col:
                    start = start + jnp.where(diagonal, 2.0 * scale / upper, 0.0)
                places = [(row, col, block, start)]
                if row != col:
                    places.append((col, row, block.T, start.T))
                for down, across, h_part, x_part in places:
                    at = (slice(down * TILE, (down + 1) * TILE), slice(across * TILE, (across + 1) * TILE))
                    h_high[at], h_low[at] = split(h_part)
                    x_high[at], x_low[at] = split(x_part)

        for g in every:
            end_predict(0, g)

        def newton(step, carry):
            scale = scales_ref[step]
            y = dot_three(h_high[...], h_low[...], x_high[...], x_low[...]) * (-scale)
            same = (lax.broadcasted_iota(jnp.int32, (filt, filt), 0)
                    == lax.broadcasted_iota(jnp.int32, (filt, filt), 1))
            y_high[...], y_low[...] = split(y + jnp.where(same, 2.0, 0.0))
            x = dot_three(x_high[...], x_low[...], y_high[...], y_low[...]) * scale
            x_high[...], x_low[...] = split(x)
            return carry

        lax.fori_loop(1, len(scales), newton, 0)

        stages = []
        for step in range(ITERS):
            stages += [
                lambda g, step=step: solve(step, g),
                lambda g, step=step: use_weights(step, g),
                lambda g, step=step: middle_predict(step + 1, g),
                lambda g, step=step: end_predict(step + 1, g),
            ]
        for tick in range(len(stages) + len(groups) - 1):
            for g in every:
                if 0 <= tick - g < len(stages):
                    stages[tick - g](g)
        for wait_sent in unsent:
            wait_sent()

    f32, bf16 = jnp.float32, jnp.bfloat16
    square = (filt, filt)
    dma = pltpu.SemaphoreType.DMA
    turns, count = ITERS + 1, len(groups)
    scratch = [
        pltpu.VMEM((filt, pos_pad), bf16),
        pltpu.VMEM((packed, TILE), f32),
        pltpu.VMEM((n_img, rows_gram, TILE), f32),
        pltpu.VMEM((packed, TILE), f32),
        pltpu.VMEM(square, bf16), pltpu.VMEM(square, bf16),
        pltpu.VMEM(square, bf16), pltpu.VMEM(square, bf16),
        pltpu.VMEM(square, bf16), pltpu.VMEM(square, bf16),
        pltpu.VMEM((turns, rows_all, pos_pad), bf16),
        pltpu.VMEM((turns, count, n_blk, chunks["blk"], pos_pad), bf16),
        pltpu.VMEM((turns, rows_all, pos_pad), bf16),
        pltpu.VMEM((ITERS, rows_all, filt), f32),
        pltpu.VMEM((ITERS, count, n_img, chunks["img"], filt), f32),
        pltpu.VMEM((ITERS, rows_all, filt), f32),
        dma((n_img,)), dma((n_img,)), dma((n_img,)), dma((n_img,)),
    ]
    scratch += [dma((turns, count, n_blk))] * 4 + [dma((ITERS, count, n_img))] * 4
    return kernel, scratch, scales, rows_all


def round_up(value, unit):
    return -(-value // unit) * unit


def make_patches(images, pos_pad):
    count = images.shape[0]
    half = SIDE // 2
    pairs = images.reshape(count, SIDE, half, 2 * CHAN)
    pairs = jnp.pad(pairs, ((0, 0), (1, 1), (1, 0), (0, 0)))
    parts = []
    for row in range(3):
        lines = pairs[:, row:row + SIDE:2]
        parts += [lines[:, :, :half], lines[:, :, 1:]]
    patches = jnp.concatenate(parts, axis=-1).reshape(count * half * half, 12 * CHAN)
    return jnp.pad(patches, ((0, pos_pad - patches.shape[0]), (0, 0)))


def solution(mesh):
    n_img, n_blk = mesh.shape["img"], mesh.shape["blk"]

    def shards(images, filters, phases, labels, weights):
        filt, pos = filters.shape[0], labels.shape[0]
        pos_pad = round_up(pos, TILE)
        groups, chunks = make_groups(n_img, n_blk)
        kernel, scratch, scales, rows_all = make_kernel(
            n_img, n_blk, filt, pos, pos_pad, pos * n_img, groups, chunks)
        patches = make_patches(images, pos_pad)
        taps = jnp.pad(filters.reshape(filt, 3, 3 * CHAN), ((0, 0), (0, 0), (CHAN, 0)))
        vmem = pl.BlockSpec(memory_space=pltpu.VMEM)
        return pl.pallas_call(
            kernel,
            out_shape=(jax.ShapeDtypeStruct((LABELS, filt), jnp.float32),
                       jax.ShapeDtypeStruct((LABELS, pos), jnp.float32)),
            in_specs=[vmem] * 5 + [pl.BlockSpec(memory_space=pltpu.SMEM)],
            out_specs=(vmem, vmem),
            scratch_shapes=scratch,
            compiler_params=pltpu.CompilerParams(
                collective_id=0, has_side_effects=True, vmem_limit_bytes=48 * 2**20),
        )(
            patches,
            taps.reshape(filt, 12 * CHAN),
            phases[:, None],
            jnp.pad(labels[None, :], ((0, 0), (0, pos_pad - pos)), constant_values=-1),
            jnp.pad(weights, ((0, rows_all - LABELS), (0, 0))),
            jnp.asarray(np.array(scales, np.float32)),
        )

    return jax.shard_map(
        shards,
        mesh=mesh,
        in_specs=(P("img", None, None), P("blk", None), P("blk"), P("img"), P(None, "blk")),
        out_specs=(P(None, "blk"), P(None, "img")),
        check_vma=False,
    )
```

```python
import math

import jax
import jax.numpy as jnp
import numpy as np
from jax import lax
from jax.experimental import pallas as pl
from jax.experimental.pallas import tpu as pltpu
from jax.sharding import PartitionSpec as P

SIDE = 28
CHAN = 64
LABELS = 150
ITERS = 2
RIDGE = 0.5
DAMPING = 0.75
TILE = 128
PANEL = 256


def cosine_coefficients(degree=6):
    nodes = np.cos((np.arange(400) + 0.5) * np.pi / 400)
    square = (nodes + 1.0) * (np.pi**2 * 1.0005) / 2
    fit = np.polynomial.chebyshev.Chebyshev.fit(square, np.sqrt(2.0) * np.cos(np.sqrt(square)), degree)
    return [float(c) for c in fit.convert(kind=np.polynomial.Polynomial).coef]


COEFFICIENTS = cosine_coefficients()
TURN_HIGH = 6.28125
TURN_LOW = 2.0 * math.pi - TURN_HIGH


def inverse_scales(lowest):
    scales = []
    while 1.0 - lowest > 1e-4:
        scale = 2.0 / (1.0 + lowest)
        scales.append(scale)
        lowest = scale * lowest * (2.0 - scale * lowest)
    return scales


def split(value):
    high = value.astype(jnp.bfloat16)
    return high, (value - high.astype(jnp.float32)).astype(jnp.bfloat16)


def dot(a, b):
    return jnp.dot(a, b, preferred_element_type=jnp.float32)


def dot_nt(a, b):
    return lax.dot_general(a, b, (((1,), (1,)), ((), ())), preferred_element_type=jnp.float32)


def dot_three(a_high, a_low, b_high, b_low):
    return dot(jnp.concatenate([a_high, a_high, a_low], 1), jnp.concatenate([b_high, b_low, b_high], 0))


def make_groups(n_img, n_blk):
    unit = math.lcm(8 * n_img, 16 * n_blk)
    chunks = {"img": unit // n_img, "blk": unit // n_blk}
    last = math.lcm(*chunks.values())
    groups = []
    first = 0
    while first < LABELS:
        rows = min(unit, round_up(LABELS - first, last))
        groups.append((first, rows))
        first += rows
    return groups, chunks


def make_kernel(n_img, n_blk, filt, pos, pos_pad, pixels, groups, chunks):
    features_all = filt * n_blk
    shrink = 1.0 / math.sqrt(features_all)
    expand = math.sqrt(features_all)
    tiles = filt // TILE
    packed = tiles * (tiles + 1) // 2 * TILE
    rows_gram = packed // n_img
    rows_all = sum(rows for _, rows in groups)
    upper = (RIDGE + 2.0 * filt) * pixels
    scales = inverse_scales(RIDGE * pixels / upper)

    def kernel(
        patches_ref, filters_ref, phases_ref, labels_ref, weights_ref, scales_ref,
        out_weights, out_residual,
        feat, gram, gram_in, gram_all, h_high, h_low, x_high, x_low, y_high, y_low,
        part, part_in, part_all, proj, proj_in, w_all,
        gram_s, gram_r, gram_all_s, gram_all_r,
        part_s, part_r, part_all_s, part_all_r,
        proj_s, proj_r, w_s, w_r,
    ):
        place = {"img": lax.axis_index("img"), "blk": lax.axis_index("blk")}
        size = {"img": n_img, "blk": n_blk}
        barrier = pltpu.get_barrier_semaphore()

        def each_peer(axis, body, owners=None):
            me, n = place[axis], size[axis]
            stride = 1 if owners is None else n // owners

            def one(step, carry):
                peer = lax.rem(me + step, n)
                if owners is None or owners == n:
                    body(step, peer, peer)
                else:
                    @pl.when((lax.rem(peer, stride) == 0) & (peer < stride * owners))
                    def _():
                        body(step, peer, peer // stride)
                return carry

            lax.fori_loop(1, n, one, 0)

        def if_owner(axis, owners, body):
            me, n = place[axis], size[axis]
            stride = n // owners
            if owners == n:
                body(me)
            else:
                @pl.when((lax.rem(me, stride) == 0) & (me < stride * owners))
                def _():
                    body(me // stride)

        for axis in size:
            each_peer(axis, lambda step, peer, owner: pl.semaphore_signal(
                barrier, inc=1, device_id={axis: peer}, device_id_type=pl.DeviceIdType.MESH))

        unsent = []

        def span(first, owner, rows):
            return pl.ds(pl.multiple_of(first + owner * rows, 8), rows)

        def scatter(axis, first, rows, owners, source, target, send, recv):
            def copy(step, peer, owner, slot):
                return pltpu.make_async_remote_copy(
                    src_ref=source.at[span(first, owner, rows)],
                    dst_ref=target.at[slot],
                    send_sem=send.at[step], recv_sem=recv.at[slot],
                    device_id={axis: peer}, device_id_type=pl.DeviceIdType.MESH)

            def start():
                me = place[axis]
                each_peer(axis, lambda step, peer, owner: copy(step, peer, owner, me).start(), owners)

                def keep(owner):
                    target[me] = source[span(first, owner, rows), :]

                if_owner(axis, owners, keep)
                unsent.append(lambda: each_peer(
                    axis, lambda step, peer, owner: copy(step, peer, owner, me).wait_send(), owners))

            def wait():
                each_peer(axis, lambda step, peer, owner: copy(step, peer, 0, peer).wait_recv())

            return start, wait

        def gather(axis, first, rows, owners, whole, send, recv):
            def copy(step, peer, owner):
                at = whole.at[span(first, owner, rows)]
                return pltpu.make_async_remote_copy(
                    src_ref=at, dst_ref=at,
                    send_sem=send.at[step], recv_sem=recv.at[owner],
                    device_id={axis: peer}, device_id_type=pl.DeviceIdType.MESH)

            def start(value):
                def share(mine):
                    whole[span(first, mine, rows), :] = value(mine)
                    each_peer(axis, lambda step, peer, owner: copy(step, peer, mine).start())

                if_owner(axis, owners, share)
                unsent.append(lambda: if_owner(axis, owners, lambda mine: each_peer(
                    axis, lambda step, peer, owner: copy(step, peer, mine).wait_send())))

            def wait():
                each_peer(axis, lambda step, peer, owner: copy(step, peer, owner).wait_recv(), owners)

            return start, wait

        for left in range(0, pos_pad, PANEL):
            here = slice(left, min(left + PANEL, pos_pad))
            angle = dot_nt(filters_ref[...], patches_ref[here, :]) + phases_ref[...]
            turns = jnp.floor(angle * (0.5 / math.pi) + 0.5)
            angle = (angle - turns * TURN_HIGH) - turns * TURN_LOW
            square = angle * angle
            value = jnp.full_like(square, COEFFICIENTS[-1])
            for coefficient in COEFFICIENTS[-2::-1]:
                value = value * square + coefficient
            if here.stop > pos:
                inside = lax.broadcasted_iota(jnp.int32, value.shape, 1) < pos - left
                value = jnp.where(inside, value, 0.0)
            feat[:, here] = value.astype(jnp.bfloat16)

        def spot_of(row, col):
            return slice((row * (row + 1) // 2 + col) * TILE, (row * (row + 1) // 2 + col + 1) * TILE)

        for left in range(0, filt, PANEL):
            block = dot_nt(feat[left:, :], feat[left:left + PANEL, :])
            for row in range(left // TILE, tiles):
                for col in range(left // TILE, min(left + PANEL, filt) // TILE):
                    if col <= row:
                        gram[spot_of(row, col), :] = block[
                            row * TILE - left:(row + 1) * TILE - left, col * TILE - left:(col + 1) * TILE - left]

        pl.semaphore_wait(barrier, n_img - 1 + n_blk - 1)
        gram_scatter = scatter("img", 0, rows_gram, n_img, gram, gram_in, gram_s, gram_r)
        gram_gather = gather("img", 0, rows_gram, n_img, gram_all, gram_all_s, gram_all_r)
        gram_scatter[0]()

        def transfers(axis, turn, g, source, target, whole, sems):
            first, rows = groups[g]
            chunk = chunks[axis]
            at = (turn, g)
            return (scatter(axis, first, chunk, rows // chunk, source.at[turn], target.at[at],
                            sems[0].at[at], sems[1].at[at])
                    + gather(axis, first, chunk, rows // chunk, whole.at[turn],
                             sems[2].at[at], sems[3].at[at]))

        def predict_transfers(turn, g):
            return transfers("blk", turn, g, part, part_in, part_all,
                             (part_s, part_r, part_all_s, part_all_r))

        def project_transfers(step, g):
            return transfers("img", step, g, proj, proj_in, w_all, (proj_s, proj_r, w_s, w_r))

        def rows_of(g):
            first, rows = groups[g]
            return slice(first, first + rows)

        def begin_predict(turn, g, weight_now):
            value = shrink * dot(weight_now.astype(jnp.bfloat16), feat[...])
            part[turn, rows_of(g), :] = value.astype(jnp.bfloat16)
            predict_transfers(turn, g)[0]()

        def middle_predict(turn, g):
            _, wait, share, _ = predict_transfers(turn, g)
            if_owner("blk", groups[g][1] // chunks["blk"], lambda mine: wait())
            share(lambda mine: jnp.sum(part_in[turn, g].astype(jnp.float32), axis=0).astype(jnp.bfloat16))

        def end_predict(turn, g):
            predict_transfers(turn, g)[3]()
            first, rows = groups[g]
            classes = lax.broadcasted_iota(jnp.int32, (rows, pos_pad), 0) + first
            targets = jnp.where(labels_ref[...] == classes, 1.0, 0.0)
            residual = targets - part_all[turn, rows_of(g), :].astype(jnp.float32)
            if turn < ITERS:
                proj[turn, rows_of(g), :] = dot_nt(residual.astype(jnp.bfloat16), feat[...])
                project_transfers(turn, g)[0]()
            else:
                end = min(first + rows, LABELS)
                out_residual[first:end, :] = residual[:end - first, :pos]

        def solve(step, g):
            _, wait, share, _ = project_transfers(step, g)

            def weight_next(mine):
                here = span(groups[g][0], mine, chunks["img"])
                before = weights_ref[here, :] if step == 0 else w_all[step - 1, here, :]
                total = jnp.sum(proj_in[step, g], axis=0)
                p_high = total.astype(jnp.bfloat16)
                high = p_high.astype(jnp.float32)
                both = jnp.concatenate([high, total - high], 0).astype(jnp.bfloat16)
                change = dot(both, x_high[last])
                rows = total.shape[0]
                change = change[:rows] + (change[rows:] + dot(p_high, x_low[last]))
                return before + DAMPING * (expand * change)

            if_owner("img", groups[g][1] // chunks["img"], lambda mine: wait())
            share(weight_next)

        def use_weights(step, g):
            project_transfers(step, g)[3]()
            begin_predict(step + 1, g, w_all[step, rows_of(g), :])
            if step == ITERS - 1:
                first, rows = groups[g]
                end = min(first + rows, LABELS)
                out_weights[first:end, :] = w_all[step, first:end, :]

        every = range(len(groups))
        for g in every:
            begin_predict(0, g, weights_ref[rows_of(g), :])
        gram_scatter[1]()
        gram_gather[0](lambda mine: jnp.sum(gram_in[...], axis=0))
        for g in every:
            middle_predict(0, g)
        gram_gather[1]()

        diagonal = (lax.broadcasted_iota(jnp.int32, (TILE, TILE), 0)
                    == lax.broadcasted_iota(jnp.int32, (TILE, TILE), 1))
        scale = scales[0]
        for row in range(tiles):
            for col in range(row + 1):
                block = gram_all[spot_of(row, col), :]
                if row == col:
                    block = block + jnp.where(diagonal, RIDGE * pixels, 0.0)
                start = block * (-scale * scale / upper / upper)
                if row == col:
                    start = start + jnp.where(diagonal, 2.0 * scale / upper, 0.0)
                places = [(row, col, block, start)]
                if row != col:
                    places.append((col, row, block.T, start.T))
                for down, across, h_part, x_part in places:
                    at = (slice(down * TILE, (down + 1) * TILE), slice(across * TILE, (across + 1) * TILE))
                    h_high[at], h_low[at] = split(h_part)
                    at = (1,) + at
                    x_high[at], x_low[at] = split(x_part)

        def newton(step, carry):
            scale = scales_ref[step]
            now, later = lax.rem(step, 2), lax.rem(step + 1, 2)
            for left in range(0, filt, PANEL):
                here = slice(left, left + PANEL)
                y = dot_three(h_high[...], h_low[...], x_high[now, :, here], x_low[now, :, here])
                same = (lax.broadcasted_iota(jnp.int32, y.shape, 0)
                        == lax.broadcasted_iota(jnp.int32, y.shape, 1) + left)
                y_high[:, here], y_low[:, here] = split(jnp.where(same, 2.0, 0.0) - scale * y)
            for left in range(0, filt, PANEL):
                here = slice(left, left + PANEL)
                x = dot_three(x_high[now], x_low[now], y_high[:, here], y_low[:, here])
                x_high[later, :, here], x_low[later, :, here] = split(scale * x)
            return carry

        for g in every:
            end_predict(0, g)
        lax.fori_loop(1, len(scales), newton, 0)
        last = len(scales) % 2

        stages = []
        for step in range(ITERS):
            stages += [
                lambda g, step=step: solve(step, g),
                lambda g, step=step: use_weights(step, g),
                lambda g, step=step: middle_predict(step + 1, g),
                lambda g, step=step: end_predict(step + 1, g),
            ]
        for tick in range(len(stages) + len(groups) - 1):
            for g in every:
                if 0 <= tick - g < len(stages):
                    stages[tick - g](g)
        for wait_sent in unsent:
            wait_sent()

    f32, bf16 = jnp.float32, jnp.bfloat16
    square = (filt, filt)
    dma = pltpu.SemaphoreType.DMA
    turns, count = ITERS + 1, len(groups)
    scratch = [
        pltpu.VMEM((filt, pos_pad), bf16),
        pltpu.VMEM((packed, TILE), f32),
        pltpu.VMEM((n_img, rows_gram, TILE), f32),
        pltpu.VMEM((packed, TILE), f32),
        pltpu.VMEM(square, bf16), pltpu.VMEM(square, bf16),
        pltpu.VMEM((2,) + square, bf16), pltpu.VMEM((2,) + square, bf16),
        pltpu.VMEM(square, bf16), pltpu.VMEM(square, bf16),
        pltpu.VMEM((turns, rows_all, pos_pad), bf16),
        pltpu.VMEM((turns, count, n_blk, chunks["blk"], pos_pad), bf16),
        pltpu.VMEM((turns, rows_all, pos_pad), bf16),
        pltpu.VMEM((ITERS, rows_all, filt), f32),
        pltpu.VMEM((ITERS, count, n_img, chunks["img"], filt), f32),
        pltpu.VMEM((ITERS, rows_all, filt), f32),
        dma((n_img,)), dma((n_img,)), dma((n_img,)), dma((n_img,)),
    ]
    scratch += [dma((turns, count, n_blk))] * 4 + [dma((ITERS, count, n_img))] * 4
    return kernel, scratch, scales, rows_all


def round_up(value, unit):
    return -(-value // unit) * unit


def make_patches(images, pos_pad):
    count = images.shape[0]
    half = SIDE // 2
    pairs = images.reshape(count, SIDE, half, 2 * CHAN)
    pairs = jnp.pad(pairs, ((0, 0), (1, 1), (1, 0), (0, 0)))
    parts = []
    for row in range(3):
        lines = pairs[:, row:row + SIDE:2]
        parts += [lines[:, :, :half], lines[:, :, 1:]]
    patches = jnp.concatenate(parts, axis=-1).reshape(count * half * half, 12 * CHAN)
    return jnp.pad(patches, ((0, pos_pad - patches.shape[0]), (0, 0)))


def solution(mesh):
    n_img, n_blk = mesh.shape["img"], mesh.shape["blk"]

    def shards(images, filters, phases, labels, weights):
        filt, pos = filters.shape[0], labels.shape[0]
        pos_pad = round_up(pos, TILE)
        groups, chunks = make_groups(n_img, n_blk)
        kernel, scratch, scales, rows_all = make_kernel(
            n_img, n_blk, filt, pos, pos_pad, pos * n_img, groups, chunks)
        patches = make_patches(images, pos_pad)
        taps = jnp.pad(filters.reshape(filt, 3, 3 * CHAN), ((0, 0), (0, 0), (CHAN, 0)))
        vmem = pl.BlockSpec(memory_space=pltpu.VMEM)
        return pl.pallas_call(
            kernel,
            out_shape=(jax.ShapeDtypeStruct((LABELS, filt), jnp.float32),
                       jax.ShapeDtypeStruct((LABELS, pos), jnp.float32)),
            in_specs=[vmem] * 5 + [pl.BlockSpec(memory_space=pltpu.SMEM)],
            out_specs=(vmem, vmem),
            scratch_shapes=scratch,
            compiler_params=pltpu.CompilerParams(
                collective_id=0, has_side_effects=True, vmem_limit_bytes=48 * 2**20),
        )(
            patches,
            taps.reshape(filt, 12 * CHAN),
            phases[:, None],
            jnp.pad(labels[None, :], ((0, 0), (0, pos_pad - pos)), constant_values=-1),
            jnp.pad(weights, ((0, rows_all - LABELS), (0, 0))),
            jnp.asarray(np.array(scales, np.float32)),
        )

    return jax.shard_map(
        shards,
        mesh=mesh,
        in_specs=(P("img", None, None), P("blk", None), P("blk"), P("img"), P(None, "blk")),
        out_specs=(P(None, "blk"), P(None, "img")),
        check_vma=False,
    )
```

```python
import math

import jax
import jax.numpy as jnp
import numpy as np
from jax import lax
from jax.experimental import pallas as pl
from jax.experimental.pallas import tpu as pltpu
from jax.sharding import PartitionSpec as P

SIDE = 28
CHAN = 64
LABELS = 150
ITERS = 2
RIDGE = 0.5
DAMPING = 0.75
TILE = 128
PANEL = 256


def cosine_coefficients(degree=6):
    nodes = np.cos((np.arange(400) + 0.5) * np.pi / 400)
    square = (nodes + 1.0) * (np.pi**2 * 1.0005) / 2
    fit = np.polynomial.chebyshev.Chebyshev.fit(square, np.sqrt(2.0) * np.cos(np.sqrt(square)), degree)
    return [float(c) for c in fit.convert(kind=np.polynomial.Polynomial).coef]


COEFFICIENTS = cosine_coefficients()
TURN_HIGH = 6.28125
TURN_LOW = 2.0 * math.pi - TURN_HIGH


def inverse_scales(lowest):
    scales = []
    while 1.0 - lowest > 1e-4:
        scale = 2.0 / (1.0 + lowest)
        scales.append(scale)
        lowest = scale * lowest * (2.0 - scale * lowest)
    return scales


def split(value):
    high = value.astype(jnp.bfloat16)
    return high, (value - high.astype(jnp.float32)).astype(jnp.bfloat16)


def dot(a, b):
    return jnp.dot(a, b, preferred_element_type=jnp.float32)


def dot_nt(a, b):
    return lax.dot_general(a, b, (((1,), (1,)), ((), ())), preferred_element_type=jnp.float32)


def dot_three(a_high, a_low, b_high, b_low):
    return dot(jnp.concatenate([a_high, a_high, a_low], 1), jnp.concatenate([b_high, b_low, b_high], 0))


def make_groups(n_img, n_blk):
    unit = math.lcm(8 * n_img, 16 * n_blk)
    chunks = {"img": unit // n_img, "blk": unit // n_blk}
    last = math.lcm(*chunks.values())
    groups = []
    first = 0
    while first < LABELS:
        rows = min(unit, round_up(LABELS - first, last))
        groups.append((first, rows))
        first += rows
    return groups, chunks


def make_kernel(n_img, n_blk, filt, pos, pos_pad, pixels, groups, chunks):
    features_all = filt * n_blk
    shrink = 1.0 / math.sqrt(features_all)
    expand = math.sqrt(features_all)
    tiles = filt // TILE
    packed = tiles * (tiles + 1) // 2 * TILE
    rows_gram = packed // n_img
    rows_all = sum(rows for _, rows in groups)
    upper = (RIDGE + 2.0 * filt) * pixels
    scales = inverse_scales(RIDGE * pixels / upper)

    def kernel(
        patches_ref, filters_ref, phases_ref, labels_ref, weights_ref, scales_ref,
        out_weights, out_residual,
        feat, gram, gram_in, gram_all, h_high, h_low, x_high, x_low, y_high, y_low,
        part, part_in, part_all, proj, proj_in, w_all,
        gram_s, gram_r, gram_all_s, gram_all_r,
        part_s, part_r, part_all_s, part_all_r,
        proj_s, proj_r, w_s, w_r,
    ):
        place = {"img": lax.axis_index("img"), "blk": lax.axis_index("blk")}
        size = {"img": n_img, "blk": n_blk}
        barrier = pltpu.get_barrier_semaphore()

        def each_peer(axis, body, owners=None):
            me, n = place[axis], size[axis]
            stride = 1 if owners is None else n // owners

            def one(step, carry):
                peer = lax.rem(me + step, n)
                if owners is None or owners == n:
                    body(step, peer, peer)
                else:
                    @pl.when((lax.rem(peer, stride) == 0) & (peer < stride * owners))
                    def _():
                        body(step, peer, peer // stride)
                return carry

            lax.fori_loop(1, n, one, 0)

        def if_owner(axis, owners, body):
            me, n = place[axis], size[axis]
            stride = n // owners
            if owners == n:
                body(me)
            else:
                @pl.when((lax.rem(me, stride) == 0) & (me < stride * owners))
                def _():
                    body(me // stride)

        for axis in size:
            each_peer(axis, lambda step, peer, owner: pl.semaphore_signal(
                barrier, inc=1, device_id={axis: peer}, device_id_type=pl.DeviceIdType.MESH))

        unsent = []

        def span(first, owner, rows):
            return pl.ds(pl.multiple_of(first + owner * rows, 8), rows)

        def scatter(axis, first, rows, owners, source, target, send, recv):
            def copy(step, peer, owner, slot):
                return pltpu.make_async_remote_copy(
                    src_ref=source.at[span(first, owner, rows)],
                    dst_ref=target.at[slot],
                    send_sem=send.at[step], recv_sem=recv.at[slot],
                    device_id={axis: peer}, device_id_type=pl.DeviceIdType.MESH)

            def start():
                me = place[axis]
                each_peer(axis, lambda step, peer, owner: copy(step, peer, owner, me).start(), owners)

                def keep(owner):
                    target[me] = source[span(first, owner, rows), :]

                if_owner(axis, owners, keep)
                unsent.append(lambda: each_peer(
                    axis, lambda step, peer, owner: copy(step, peer, owner, me).wait_send(), owners))

            def wait():
                each_peer(axis, lambda step, peer, owner: copy(step, peer, 0, peer).wait_recv())

            return start, wait

        def gather(axis, first, rows, owners, whole, send, recv):
            def copy(step, peer, owner):
                at = whole.at[span(first, owner, rows)]
                return pltpu.make_async_remote_copy(
                    src_ref=at, dst_ref=at,
                    send_sem=send.at[step], recv_sem=recv.at[owner],
                    device_id={axis: peer}, device_id_type=pl.DeviceIdType.MESH)

            def start(value):
                def share(mine):
                    whole[span(first, mine, rows), :] = value(mine)
                    each_peer(axis, lambda step, peer, owner: copy(step, peer, mine).start())

                if_owner(axis, owners, share)
                unsent.append(lambda: if_owner(axis, owners, lambda mine: each_peer(
                    axis, lambda step, peer, owner: copy(step, peer, mine).wait_send())))

            def wait():
                each_peer(axis, lambda step, peer, owner: copy(step, peer, owner).wait_recv(), owners)

            return start, wait

        for top in range(0, filt, PANEL):
            here = slice(top, top + PANEL)
            angle = dot_nt(filters_ref[here, :], patches_ref[...]) + phases_ref[here, :]
            turns = jnp.floor(angle * (0.5 / math.pi) + 0.5)
            angle = (angle - turns * TURN_HIGH) - turns * TURN_LOW
            square = angle * angle
            value = jnp.full_like(square, COEFFICIENTS[-1])
            for coefficient in COEFFICIENTS[-2::-1]:
                value = value * square + coefficient
            inside = lax.broadcasted_iota(jnp.int32, value.shape, 1) < pos
            feat[here, :] = jnp.where(inside, value, 0.0).astype(jnp.bfloat16)

        def spot_of(row, col):
            return slice((row * (row + 1) // 2 + col) * TILE, (row * (row + 1) // 2 + col + 1) * TILE)

        for top in range(0, filt, PANEL):
            block = dot_nt(feat[top:top + PANEL, :], feat[:top + PANEL, :])
            for row in range(top // TILE, (top + PANEL) // TILE):
                for col in range(row + 1):
                    gram[spot_of(row, col), :] = block[
                        row * TILE - top:(row + 1) * TILE - top, col * TILE:(col + 1) * TILE]

        pl.semaphore_wait(barrier, n_img - 1 + n_blk - 1)
        gram_scatter = scatter("img", 0, rows_gram, n_img, gram, gram_in, gram_s, gram_r)
        gram_gather = gather("img", 0, rows_gram, n_img, gram_all, gram_all_s, gram_all_r)
        gram_scatter[0]()

        def transfers(axis, turn, g, source, target, whole, sems):
            first, rows = groups[g]
            chunk = chunks[axis]
            at = (turn, g)
            return (scatter(axis, first, chunk, rows // chunk, source.at[turn], target.at[at],
                            sems[0].at[at], sems[1].at[at])
                    + gather(axis, first, chunk, rows // chunk, whole.at[turn],
                             sems[2].at[at], sems[3].at[at]))

        def predict_transfers(turn, g):
            return transfers("blk", turn, g, part, part_in, part_all,
                             (part_s, part_r, part_all_s, part_all_r))

        def project_transfers(step, g):
            return transfers("img", step, g, proj, proj_in, w_all, (proj_s, proj_r, w_s, w_r))

        def rows_of(g):
            first, rows = groups[g]
            return slice(first, first + rows)

        def begin_predict(turn, g, weight_now):
            value = shrink * dot(weight_now.astype(jnp.bfloat16), feat[...])
            part[turn, rows_of(g), :] = value.astype(jnp.bfloat16)
            predict_transfers(turn, g)[0]()

        def middle_predict(turn, g):
            _, wait, share, _ = predict_transfers(turn, g)
            if_owner("blk", groups[g][1] // chunks["blk"], lambda mine: wait())
            share(lambda mine: jnp.sum(part_in[turn, g].astype(jnp.float32), axis=0).astype(jnp.bfloat16))

        def end_predict(turn, g):
            predict_transfers(turn, g)[3]()
            first, rows = groups[g]
            classes = lax.broadcasted_iota(jnp.int32, (rows, pos_pad), 0) + first
            targets = jnp.where(labels_ref[...] == classes, 1.0, 0.0)
            residual = targets - part_all[turn, rows_of(g), :].astype(jnp.float32)
            if turn < ITERS:
                proj[turn, rows_of(g), :] = dot_nt(residual.astype(jnp.bfloat16), feat[...])
                project_transfers(turn, g)[0]()
            else:
                end = min(first + rows, LABELS)
                out_residual[first:end, :] = residual[:end - first, :pos]

        def solve(step, g):
            _, wait, share, _ = project_transfers(step, g)

            def weight_next(mine):
                here = span(groups[g][0], mine, chunks["img"])
                before = weights_ref[here, :] if step == 0 else w_all[step - 1, here, :]
                total = jnp.sum(proj_in[step, g], axis=0)
                p_high = total.astype(jnp.bfloat16)
                high = p_high.astype(jnp.float32)
                both = jnp.concatenate([high, total - high], 0).astype(jnp.bfloat16)
                change = dot(both, x_high[...])
                rows = total.shape[0]
                change = change[:rows] + (change[rows:] + dot(p_high, x_low[...]))
                return before + DAMPING * (expand * change)

            if_owner("img", groups[g][1] // chunks["img"], lambda mine: wait())
            share(weight_next)

        def use_weights(step, g):
            project_transfers(step, g)[3]()
            begin_predict(step + 1, g, w_all[step, rows_of(g), :])
            if step == ITERS - 1:
                first, rows = groups[g]
                end = min(first + rows, LABELS)
                out_weights[first:end, :] = w_all[step, first:end, :]

        every = range(len(groups))
        for g in every:
            begin_predict(0, g, weights_ref[rows_of(g), :])
        gram_scatter[1]()
        gram_gather[0](lambda mine: jnp.sum(gram_in[...], axis=0))
        for g in every:
            middle_predict(0, g)
        gram_gather[1]()

        diagonal = (lax.broadcasted_iota(jnp.int32, (TILE, TILE), 0)
                    == lax.broadcasted_iota(jnp.int32, (TILE, TILE), 1))
        scale = scales[0]
        for row in range(tiles):
            for col in range(row + 1):
                block = gram_all[spot_of(row, col), :]
                if row == col:
                    block = block + jnp.where(diagonal, RIDGE * pixels, 0.0)
                start = block * (-scale * scale / upper / upper)
                if row == col:
                    start = start + jnp.where(diagonal, 2.0 * scale / upper, 0.0)
                places = [(row, col, block, start)]
                if row != col:
                    places.append((col, row, block.T, start.T))
                for down, across, h_part, x_part in places:
                    at = (slice(down * TILE, (down + 1) * TILE), slice(across * TILE, (across + 1) * TILE))
                    h_high[at], h_low[at] = split(h_part)
                    x_high[at], x_low[at] = split(x_part)

        def newton(step, carry):
            scale = scales_ref[step]
            for top in range(0, filt, PANEL):
                here = slice(top, top + PANEL)
                y = dot_three(h_high[here, :], h_low[here, :], x_high[...], x_low[...])
                same = (lax.broadcasted_iota(jnp.int32, y.shape, 0) + top
                        == lax.broadcasted_iota(jnp.int32, y.shape, 1))
                y_high[here, :], y_low[here, :] = split(jnp.where(same, 2.0, 0.0) - scale * y)
            for top in range(0, filt, PANEL):
                here = slice(top, top + PANEL)
                x = dot_three(x_high[here, :], x_low[here, :], y_high[...], y_low[...])
                x_high[here, :], x_low[here, :] = split(scale * x)
            return carry

        for g in every:
            end_predict(0, g)
        lax.fori_loop(1, len(scales), newton, 0)

        stages = []
        for step in range(ITERS):
            stages += [
                lambda g, step=step: solve(step, g),
                lambda g, step=step: use_weights(step, g),
                lambda g, step=step: middle_predict(step + 1, g),
                lambda g, step=step: end_predict(step + 1, g),
            ]
        for tick in range(len(stages) + len(groups) - 1):
            for g in every:
                if 0 <= tick - g < len(stages):
                    stages[tick - g](g)
        for wait_sent in unsent:
            wait_sent()

    f32, bf16 = jnp.float32, jnp.bfloat16
    square = (filt, filt)
    dma = pltpu.SemaphoreType.DMA
    turns, count = ITERS + 1, len(groups)
    scratch = [
        pltpu.VMEM((filt, pos_pad), bf16),
        pltpu.VMEM((packed, TILE), f32),
        pltpu.VMEM((n_img, rows_gram, TILE), f32),
        pltpu.VMEM((packed, TILE), f32),
        pltpu.VMEM(square, bf16), pltpu.VMEM(square, bf16),
        pltpu.VMEM(square, bf16), pltpu.VMEM(square, bf16),
        pltpu.VMEM(square, bf16), pltpu.VMEM(square, bf16),
        pltpu.VMEM((turns, rows_all, pos_pad), bf16),
        pltpu.VMEM((turns, count, n_blk, chunks["blk"], pos_pad), bf16),
        pltpu.VMEM((turns, rows_all, pos_pad), bf16),
        pltpu.VMEM((ITERS, rows_all, filt), f32),
        pltpu.VMEM((ITERS, count, n_img, chunks["img"], filt), f32),
        pltpu.VMEM((ITERS, rows_all, filt), f32),
        dma((n_img,)), dma((n_img,)), dma((n_img,)), dma((n_img,)),
    ]
    scratch += [dma((turns, count, n_blk))] * 4 + [dma((ITERS, count, n_img))] * 4
    return kernel, scratch, scales, rows_all


def round_up(value, unit):
    return -(-value // unit) * unit


def make_patches(images, pos_pad):
    count = images.shape[0]
    half = SIDE // 2
    pairs = images.reshape(count, SIDE, half, 2 * CHAN)
    pairs = jnp.pad(pairs, ((0, 0), (1, 1), (1, 0), (0, 0)))
    parts = []
    for row in range(3):
        lines = pairs[:, row:row + SIDE:2]
        parts += [lines[:, :, :half], lines[:, :, 1:]]
    patches = jnp.concatenate(parts, axis=-1).reshape(count * half * half, 12 * CHAN)
    return jnp.pad(patches, ((0, pos_pad - patches.shape[0]), (0, 0)))


def solution(mesh):
    n_img, n_blk = mesh.shape["img"], mesh.shape["blk"]

    def shards(images, filters, phases, labels, weights):
        filt, pos = filters.shape[0], labels.shape[0]
        pos_pad = round_up(pos, TILE)
        groups, chunks = make_groups(n_img, n_blk)
        kernel, scratch, scales, rows_all = make_kernel(
            n_img, n_blk, filt, pos, pos_pad, pos * n_img, groups, chunks)
        patches = make_patches(images, pos_pad)
        taps = jnp.pad(filters.reshape(filt, 3, 3 * CHAN), ((0, 0), (0, 0), (CHAN, 0)))
        vmem = pl.BlockSpec(memory_space=pltpu.VMEM)
        return pl.pallas_call(
            kernel,
            out_shape=(jax.ShapeDtypeStruct((LABELS, filt), jnp.float32),
                       jax.ShapeDtypeStruct((LABELS, pos), jnp.float32)),
            in_specs=[vmem] * 5 + [pl.BlockSpec(memory_space=pltpu.SMEM)],
            out_specs=(vmem, vmem),
            scratch_shapes=scratch,
            compiler_params=pltpu.CompilerParams(
                collective_id=0, has_side_effects=True, vmem_limit_bytes=48 * 2**20),
        )(
            patches,
            taps.reshape(filt, 12 * CHAN),
            phases[:, None],
            jnp.pad(labels[None, :], ((0, 0), (0, pos_pad - pos)), constant_values=-1),
            jnp.pad(weights, ((0, rows_all - LABELS), (0, 0))),
            jnp.asarray(np.array(scales, np.float32)),
        )

    return jax.shard_map(
        shards,
        mesh=mesh,
        in_specs=(P("img", None, None), P("blk", None), P("blk"), P("img"), P(None, "blk")),
        out_specs=(P(None, "blk"), P(None, "img")),
        check_vma=False,
    )
```

```python
import math

import jax
import jax.numpy as jnp
import numpy as np
from jax import lax
from jax.experimental import pallas as pl
from jax.experimental.pallas import tpu as pltpu
from jax.sharding import PartitionSpec as P

SIDE = 28
CHAN = 64
LABELS = 150
ITERS = 2
RIDGE = 0.5
DAMPING = 0.75
TILE = 128
PANEL = 256


def cosine_coefficients(degree=6):
    nodes = np.cos((np.arange(400) + 0.5) * np.pi / 400)
    square = (nodes + 1.0) * (np.pi**2 * 1.0005) / 2
    fit = np.polynomial.chebyshev.Chebyshev.fit(square, np.sqrt(2.0) * np.cos(np.sqrt(square)), degree)
    return [float(c) for c in fit.convert(kind=np.polynomial.Polynomial).coef]


COEFFICIENTS = cosine_coefficients()
TURN_HIGH = 6.28125
TURN_LOW = 2.0 * math.pi - TURN_HIGH


def inverse_scales(lowest):
    scales = []
    while 1.0 - lowest > 1e-4:
        scale = 2.0 / (1.0 + lowest)
        scales.append(scale)
        lowest = scale * lowest * (2.0 - scale * lowest)
    return scales


def split(value):
    high = value.astype(jnp.bfloat16)
    return high, (value - high.astype(jnp.float32)).astype(jnp.bfloat16)


def dot(a, b):
    return jnp.dot(a, b, preferred_element_type=jnp.float32)


def dot_nt(a, b):
    return lax.dot_general(a, b, (((1,), (1,)), ((), ())), preferred_element_type=jnp.float32)


def dot_three(a_high, a_low, b_high, b_low):
    return dot(jnp.concatenate([a_high, a_high, a_low], 1), jnp.concatenate([b_high, b_low, b_high], 0))


def make_groups(n_img, n_blk):
    unit = math.lcm(8 * n_img, 16 * n_blk)
    chunks = {"img": unit // n_img, "blk": unit // n_blk}
    last = math.lcm(*chunks.values())
    groups = []
    first = 0
    while first < LABELS:
        rows = min(unit, round_up(LABELS - first, last))
        groups.append((first, rows))
        first += rows
    return groups, chunks


def make_kernel(n_img, n_blk, filt, pos, pos_pad, pixels, groups, chunks):
    features_all = filt * n_blk
    shrink = 1.0 / math.sqrt(features_all)
    expand = math.sqrt(features_all)
    tiles = filt // TILE
    packed = tiles * (tiles + 1) // 2 * TILE
    half = packed // 2
    rows_gram = packed // n_img
    pairs = n_img // 2
    rows_all = sum(rows for _, rows in groups)
    upper = (RIDGE + 2.0 * filt) * pixels
    scales = inverse_scales(RIDGE * pixels / upper)

    def kernel(
        patches_ref, filters_ref, phases_ref, labels_ref, weights_ref, scales_ref,
        out_weights, out_residual,
        feat, gram, gram_half, gram_sum, gram_in, gram_all, h_high, h_low, x_high, x_low, y_high, y_low,
        part, part_in, part_all, proj, proj_in, w_all,
        gram_s, gram_r, gram_all_s, gram_all_r,
        part_s, part_r, part_all_s, part_all_r,
        proj_s, proj_r, w_s, w_r,
    ):
        place = {"img": lax.axis_index("img"), "blk": lax.axis_index("blk")}
        size = {"img": n_img, "blk": n_blk}
        barrier = pltpu.get_barrier_semaphore()

        def each_peer(axis, body, owners=None):
            me, n = place[axis], size[axis]
            stride = 1 if owners is None else n // owners

            def one(step, carry):
                peer = lax.rem(me + step, n)
                if owners is None or owners == n:
                    body(step, peer, peer)
                else:
                    @pl.when((lax.rem(peer, stride) == 0) & (peer < stride * owners))
                    def _():
                        body(step, peer, peer // stride)
                return carry

            if n <= 8:
                for step in range(1, n):
                    one(step, 0)
            else:
                lax.fori_loop(1, n, one, 0)

        def if_owner(axis, owners, body):
            me, n = place[axis], size[axis]
            stride = n // owners
            if owners == n:
                body(me)
            else:
                @pl.when((lax.rem(me, stride) == 0) & (me < stride * owners))
                def _():
                    body(me // stride)

        for axis in size:
            each_peer(axis, lambda step, peer, owner: pl.semaphore_signal(
                barrier, inc=1, device_id={axis: peer}, device_id_type=pl.DeviceIdType.MESH))

        unsent = []

        def span(first, owner, rows):
            return pl.ds(pl.multiple_of(first + owner * rows, 8), rows)

        def scatter(axis, first, rows, owners, source, target, send, recv):
            def copy(step, peer, owner, slot):
                return pltpu.make_async_remote_copy(
                    src_ref=source.at[span(first, owner, rows)],
                    dst_ref=target.at[slot],
                    send_sem=send.at[step], recv_sem=recv.at[slot],
                    device_id={axis: peer}, device_id_type=pl.DeviceIdType.MESH)

            def start():
                me = place[axis]
                each_peer(axis, lambda step, peer, owner: copy(step, peer, owner, me).start(), owners)

                def keep(owner):
                    target[me] = source[span(first, owner, rows), :]

                if_owner(axis, owners, keep)
                unsent.append(lambda: each_peer(
                    axis, lambda step, peer, owner: copy(step, peer, owner, me).wait_send(), owners))

            def wait():
                each_peer(axis, lambda step, peer, owner: copy(step, peer, 0, peer).wait_recv())

            return start, wait

        def gather(axis, first, rows, owners, whole, send, recv):
            def copy(step, peer, owner):
                at = whole.at[span(first, owner, rows)]
                return pltpu.make_async_remote_copy(
                    src_ref=at, dst_ref=at,
                    send_sem=send.at[step], recv_sem=recv.at[owner],
                    device_id={axis: peer}, device_id_type=pl.DeviceIdType.MESH)

            def start(value):
                def share(mine):
                    whole[span(first, mine, rows), :] = value(mine)
                    each_peer(axis, lambda step, peer, owner: copy(step, peer, mine).start())

                if_owner(axis, owners, share)
                unsent.append(lambda: if_owner(axis, owners, lambda mine: each_peer(
                    axis, lambda step, peer, owner: copy(step, peer, mine).wait_send())))

            def wait():
                each_peer(axis, lambda step, peer, owner: copy(step, peer, owner).wait_recv(), owners)

            return start, wait

        for top in range(0, filt, PANEL):
            here = slice(top, top + PANEL)
            angle = dot_nt(filters_ref[here, :], patches_ref[...]) + phases_ref[here, :]
            turns = jnp.floor(angle * (0.5 / math.pi) + 0.5)
            angle = (angle - turns * TURN_HIGH) - turns * TURN_LOW
            square = angle * angle
            value = jnp.full_like(square, COEFFICIENTS[-1])
            for coefficient in COEFFICIENTS[-2::-1]:
                value = value * square + coefficient
            inside = lax.broadcasted_iota(jnp.int32, value.shape, 1) < pos
            feat[here, :] = jnp.where(inside, value, 0.0).astype(jnp.bfloat16)

        def spot_of(row, col):
            return slice((row * (row + 1) // 2 + col) * TILE, (row * (row + 1) // 2 + col + 1) * TILE)

        for top in range(0, filt, PANEL):
            block = dot_nt(feat[top:top + PANEL, :], feat[:top + PANEL, :])
            for row in range(top // TILE, (top + PANEL) // TILE):
                for col in range(row + 1):
                    gram[spot_of(row, col), :] = block[
                        row * TILE - top:(row + 1) * TILE - top, col * TILE:(col + 1) * TILE]

        pl.semaphore_wait(barrier, n_img - 1 + n_blk - 1)

        number, side = place["img"] // 2, lax.rem(place["img"], 2)
        other = place["img"] + 1 - 2 * side

        def to_device(source, target, send, recv, device):
            return pltpu.make_async_remote_copy(
                src_ref=source, dst_ref=target, send_sem=send, recv_sem=recv,
                device_id={"img": device}, device_id_type=pl.DeviceIdType.MESH)

        def each_pair(body):
            for step in range(1, pairs):
                peer = lax.rem(number + step, pairs)
                body(step, peer, 2 * peer + side)

        def gram_chunk(which):
            return gram_all.at[span(side * half, which, rows_gram)]

        def halves(from_side):
            return to_device(gram.at[span(0, from_side, half)], gram_half, gram_s.at[0], gram_r.at[0], other)

        def to_owner(step, peer, slot, device):
            return to_device(gram_sum.at[span(0, peer, rows_gram)], gram_in.at[slot],
                             gram_s.at[step], gram_r.at[1 + slot], device)

        def to_all(step, chunk, device):
            return to_device(gram_chunk(chunk), gram_chunk(chunk), gram_all_s.at[step], gram_all_r.at[chunk], device)

        def to_other(chunk, at_side):
            at = gram_all.at[span(at_side * half, chunk, rows_gram)]
            return to_device(at, at, gram_all_s.at[pairs + chunk], gram_all_r.at[pairs + chunk], other)

        halves(1 - side).start()

        def transfers(axis, turn, g, source, target, whole, sems):
            first, rows = groups[g]
            chunk = chunks[axis]
            at = (turn, g)
            return (scatter(axis, first, chunk, rows // chunk, source.at[turn], target.at[at],
                            sems[0].at[at], sems[1].at[at])
                    + gather(axis, first, chunk, rows // chunk, whole.at[turn],
                             sems[2].at[at], sems[3].at[at]))

        def predict_transfers(turn, g):
            return transfers("blk", turn, g, part, part_in, part_all,
                             (part_s, part_r, part_all_s, part_all_r))

        def project_transfers(step, g):
            return transfers("img", step, g, proj, proj_in, w_all, (proj_s, proj_r, w_s, w_r))

        def rows_of(g):
            first, rows = groups[g]
            return slice(first, first + rows)

        def begin_predict(turn, g, weight_now):
            value = shrink * dot(weight_now.astype(jnp.bfloat16), feat[...])
            part[turn, rows_of(g), :] = value.astype(jnp.bfloat16)
            predict_transfers(turn, g)[0]()

        def middle_predict(turn, g):
            _, wait, share, _ = predict_transfers(turn, g)
            if_owner("blk", groups[g][1] // chunks["blk"], lambda mine: wait())
            share(lambda mine: jnp.sum(part_in[turn, g].astype(jnp.float32), axis=0).astype(jnp.bfloat16))

        def end_predict(turn, g):
            predict_transfers(turn, g)[3]()
            first, rows = groups[g]
            classes = lax.broadcasted_iota(jnp.int32, (rows, pos_pad), 0) + first
            targets = jnp.where(labels_ref[...] == classes, 1.0, 0.0)
            residual = targets - part_all[turn, rows_of(g), :].astype(jnp.float32)
            if turn < ITERS:
                proj[turn, rows_of(g), :] = dot_nt(residual.astype(jnp.bfloat16), feat[...])
                project_transfers(turn, g)[0]()
            else:
                end = min(first + rows, LABELS)
                out_residual[first:end, :] = residual[:end - first, :pos]

        def solve(step, g):
            _, wait, share, _ = project_transfers(step, g)

            def weight_next(mine):
                here = span(groups[g][0], mine, chunks["img"])
                before = weights_ref[here, :] if step == 0 else w_all[step - 1, here, :]
                total = jnp.sum(proj_in[step, g], axis=0)
                p_high = total.astype(jnp.bfloat16)
                high = p_high.astype(jnp.float32)
                both = jnp.concatenate([high, total - high], 0).astype(jnp.bfloat16)
                change = dot(both, x_high[...])
                rows = total.shape[0]
                change = change[:rows] + (change[rows:] + dot(p_high, x_low[...]))
                return before + DAMPING * (expand * change)

            if_owner("img", groups[g][1] // chunks["img"], lambda mine: wait())
            share(weight_next)

        def use_weights(step, g):
            project_transfers(step, g)[3]()
            begin_predict(step + 1, g, w_all[step, rows_of(g), :])
            if step == ITERS - 1:
                first, rows = groups[g]
                end = min(first + rows, LABELS)
                out_weights[first:end, :] = w_all[step, first:end, :]

        every = range(len(groups))
        begin_predict(0, 0, weights_ref[rows_of(0), :])
        halves(side).wait_recv()
        gram_sum[...] = gram[span(0, side, half), :] + gram_half[...]
        each_pair(lambda step, peer, device: to_owner(step, peer, number, device).start())
        gram_in[number] = gram_sum[span(0, number, rows_gram), :]
        for g in every[1:]:
            begin_predict(0, g, weights_ref[rows_of(g), :])
        each_pair(lambda step, peer, device: to_owner(step, peer, peer, device).wait_recv())
        gram_chunk(number)[...] = jnp.sum(gram_in[...], axis=0)
        each_pair(lambda step, peer, device: to_all(step, number, device).start())
        to_other(number, side).start()
        for g in every:
            middle_predict(0, g)

        def pass_on(step, peer, device):
            to_all(step, peer, device).wait_recv()
            to_other(peer, side).start()

        each_pair(pass_on)
        for chunk in range(pairs):
            to_other(chunk, 1 - side).wait_recv()

        diagonal = (lax.broadcasted_iota(jnp.int32, (TILE, TILE), 0)
                    == lax.broadcasted_iota(jnp.int32, (TILE, TILE), 1))
        scale = scales[0]
        for row in range(tiles):
            for col in range(row + 1):
                block = gram_all[spot_of(row, col), :]
                if row == col:
                    block = block + jnp.where(diagonal, RIDGE * pixels, 0.0)
                start = block * (-scale * scale / upper / upper)
                if row == col:
                    start = start + jnp.where(diagonal, 2.0 * scale / upper, 0.0)
                places = [(row, col, block, start)]
                if row != col:
                    places.append((col, row, block.T, start.T))
                for down, across, h_part, x_part in places:
                    at = (slice(down * TILE, (down + 1) * TILE), slice(across * TILE, (across + 1) * TILE))
                    h_high[at], h_low[at] = split(h_part)
                    x_high[at], x_low[at] = split(x_part)

        def newton(step, carry):
            scale = scales_ref[step]
            y = dot_three(h_high[...], h_low[...], x_high[...], x_low[...])
            same = (lax.broadcasted_iota(jnp.int32, y.shape, 0)
                    == lax.broadcasted_iota(jnp.int32, y.shape, 1))
            y_high[...], y_low[...] = split(jnp.where(same, 2.0, 0.0) - scale * y)
            x = dot_three(x_high[...], x_low[...], y_high[...], y_low[...])
            x_high[...], x_low[...] = split(scale * x)
            return carry

        begun = (len(scales) + 1) // 2
        lax.fori_loop(1, begun, newton, 0)
        for g in every:
            end_predict(0, g)
        lax.fori_loop(begun, len(scales), newton, 0)

        stages = []
        for step in range(ITERS):
            stages += [
                lambda g, step=step: solve(step, g),
                lambda g, step=step: use_weights(step, g),
                lambda g, step=step: middle_predict(step + 1, g),
                lambda g, step=step: end_predict(step + 1, g),
            ]
        for tick in range(len(stages) + len(groups) - 1):
            for g in every:
                if 0 <= tick - g < len(stages):
                    stages[tick - g](g)
        for wait_sent in unsent:
            wait_sent()
        halves(1 - side).wait_send()
        each_pair(lambda step, peer, device: to_owner(step, peer, number, device).wait_send())
        each_pair(lambda step, peer, device: to_all(step, number, device).wait_send())
        for chunk in range(pairs):
            to_other(chunk, side).wait_send()

    f32, bf16 = jnp.float32, jnp.bfloat16
    square = (filt, filt)
    dma = pltpu.SemaphoreType.DMA
    turns, count = ITERS + 1, len(groups)
    scratch = [
        pltpu.VMEM((filt, pos_pad), bf16),
        pltpu.VMEM((packed, TILE), f32),
        pltpu.VMEM((half, TILE), f32),
        pltpu.VMEM((half, TILE), f32),
        pltpu.VMEM((pairs, rows_gram, TILE), f32),
        pltpu.VMEM((packed, TILE), f32),
        pltpu.VMEM(square, bf16), pltpu.VMEM(square, bf16),
        pltpu.VMEM(square, bf16), pltpu.VMEM(square, bf16),
        pltpu.VMEM(square, bf16), pltpu.VMEM(square, bf16),
        pltpu.VMEM((turns, rows_all, pos_pad), bf16),
        pltpu.VMEM((turns, count, n_blk, chunks["blk"], pos_pad), bf16),
        pltpu.VMEM((turns, rows_all, pos_pad), bf16),
        pltpu.VMEM((ITERS, rows_all, filt), f32),
        pltpu.VMEM((ITERS, count, n_img, chunks["img"], filt), f32),
        pltpu.VMEM((ITERS, rows_all, filt), f32),
        dma((n_img,)), dma((n_img,)), dma((n_img,)), dma((n_img,)),
    ]
    scratch += [dma((turns, count, n_blk))] * 4 + [dma((ITERS, count, n_img))] * 4
    return kernel, scratch, scales, rows_all


def round_up(value, unit):
    return -(-value // unit) * unit


def make_patches(images, pos_pad):
    count = images.shape[0]
    half = SIDE // 2
    pairs = images.reshape(count, SIDE, half, 2 * CHAN)
    pairs = jnp.pad(pairs, ((0, 0), (1, 1), (1, 0), (0, 0)))
    parts = []
    for row in range(3):
        lines = pairs[:, row:row + SIDE:2]
        parts += [lines[:, :, :half], lines[:, :, 1:]]
    patches = jnp.concatenate(parts, axis=-1).reshape(count * half * half, 12 * CHAN)
    return jnp.pad(patches, ((0, pos_pad - patches.shape[0]), (0, 0)))


def solution(mesh):
    n_img, n_blk = mesh.shape["img"], mesh.shape["blk"]

    def shards(images, filters, phases, labels, weights):
        filt, pos = filters.shape[0], labels.shape[0]
        pos_pad = round_up(pos, TILE)
        groups, chunks = make_groups(n_img, n_blk)
        kernel, scratch, scales, rows_all = make_kernel(
            n_img, n_blk, filt, pos, pos_pad, pos * n_img, groups, chunks)
        patches = make_patches(images, pos_pad)
        taps = jnp.pad(filters.reshape(filt, 3, 3 * CHAN), ((0, 0), (0, 0), (CHAN, 0)))
        vmem = pl.BlockSpec(memory_space=pltpu.VMEM)
        return pl.pallas_call(
            kernel,
            out_shape=(jax.ShapeDtypeStruct((LABELS, filt), jnp.float32),
                       jax.ShapeDtypeStruct((LABELS, pos), jnp.float32)),
            in_specs=[vmem] * 5 + [pl.BlockSpec(memory_space=pltpu.SMEM)],
            out_specs=(vmem, vmem),
            scratch_shapes=scratch,
            compiler_params=pltpu.CompilerParams(
                collective_id=0, has_side_effects=True, vmem_limit_bytes=48 * 2**20),
        )(
            patches,
            taps.reshape(filt, 12 * CHAN),
            phases[:, None],
            jnp.pad(labels[None, :], ((0, 0), (0, pos_pad - pos)), constant_values=-1),
            jnp.pad(weights, ((0, rows_all - LABELS), (0, 0))),
            jnp.asarray(np.array(scales, np.float32)),
        )

    return jax.shard_map(
        shards,
        mesh=mesh,
        in_specs=(P("img", None, None), P("blk", None), P("blk"), P("img"), P(None, "blk")),
        out_specs=(P(None, "blk"), P(None, "img")),
        check_vma=False,
    )
```

```python
import math

import jax
import jax.numpy as jnp
import numpy as np
from jax import lax
from jax.experimental import pallas as pl
from jax.experimental.pallas import tpu as pltpu
from jax.sharding import PartitionSpec as P

SIDE = 28
CHAN = 64
LABELS = 150
ITERS = 2
RIDGE = 0.5
DAMPING = 0.75
TILE = 128
PANEL = 256


def cosine_coefficients(degree=6):
    nodes = np.cos((np.arange(400) + 0.5) * np.pi / 400)
    square = (nodes + 1.0) * (np.pi**2 * 1.0005) / 2
    fit = np.polynomial.chebyshev.Chebyshev.fit(square, np.sqrt(2.0) * np.cos(np.sqrt(square)), degree)
    return [float(c) for c in fit.convert(kind=np.polynomial.Polynomial).coef]


COEFFICIENTS = cosine_coefficients()
TURN_HIGH = 6.28125
TURN_LOW = 2.0 * math.pi - TURN_HIGH


def inverse_scales(lowest):
    scales = []
    while 1.0 - lowest > 1e-4:
        scale = 2.0 / (1.0 + lowest)
        scales.append(scale)
        lowest = scale * lowest * (2.0 - scale * lowest)
    return scales


def split(value):
    high = value.astype(jnp.bfloat16)
    return high, (value - high.astype(jnp.float32)).astype(jnp.bfloat16)


def dot(a, b):
    return jnp.dot(a, b, preferred_element_type=jnp.float32)


def dot_nt(a, b):
    return lax.dot_general(a, b, (((1,), (1,)), ((), ())), preferred_element_type=jnp.float32)


def dot_three(a_high, a_low, b_high, b_low):
    return dot(jnp.concatenate([a_high, a_high, a_low], 1), jnp.concatenate([b_high, b_low, b_high], 0))


def make_groups(n_img, n_blk):
    unit = math.lcm(8 * n_img, 16 * n_blk)
    chunks = {"img": unit // n_img, "blk": unit // n_blk}
    last = math.lcm(*chunks.values())
    unit = max(unit // 2, last)
    groups = []
    first = 0
    while first < LABELS:
        rows = min(unit, round_up(LABELS - first, last))
        groups.append((first, rows))
        first += rows
    return groups, chunks


def make_kernel(n_img, n_blk, filt, pos, pos_pad, pixels, groups, chunks):
    features_all = filt * n_blk
    shrink = 1.0 / math.sqrt(features_all)
    expand = math.sqrt(features_all)
    tiles = filt // TILE
    packed = tiles * (tiles + 1) // 2 * TILE
    half = packed // 2
    rows_gram = packed // n_img
    pairs = n_img // 2
    rows_all = sum(rows for _, rows in groups)
    upper = (RIDGE + 2.0 * filt) * pixels
    scales = inverse_scales(RIDGE * pixels / upper)

    def kernel(
        patches_ref, filters_ref, phases_ref, labels_ref, weights_ref, scales_ref,
        out_weights, out_residual,
        feat, gram, gram_half, gram_sum, gram_in, gram_all, h_high, h_low, x_high, x_low, y_high, y_low,
        part, part_in, part_all, proj, proj_in, w_all,
        gram_s, gram_r, gram_all_s, gram_all_r,
        part_s, part_r, part_all_s, part_all_r,
        proj_s, proj_r, w_s, w_r,
    ):
        place = {"img": lax.axis_index("img"), "blk": lax.axis_index("blk")}
        size = {"img": n_img, "blk": n_blk}
        barrier = pltpu.get_barrier_semaphore()

        def each_peer(axis, body, owners=None):
            me, n = place[axis], size[axis]
            stride = 1 if owners is None else n // owners

            def one(step, carry):
                peer = lax.rem(me + step, n)
                if owners is None or owners == n:
                    body(step, peer, peer)
                else:
                    @pl.when((lax.rem(peer, stride) == 0) & (peer < stride * owners))
                    def _():
                        body(step, peer, peer // stride)
                return carry

            if n <= 8:
                for step in range(1, n):
                    one(step, 0)
            else:
                lax.fori_loop(1, n, one, 0)

        def if_owner(axis, owners, body):
            me, n = place[axis], size[axis]
            stride = n // owners
            if owners == n:
                body(me)
            else:
                @pl.when((lax.rem(me, stride) == 0) & (me < stride * owners))
                def _():
                    body(me // stride)

        for axis in size:
            each_peer(axis, lambda step, peer, owner: pl.semaphore_signal(
                barrier, inc=1, device_id={axis: peer}, device_id_type=pl.DeviceIdType.MESH))

        unsent = []

        def span(first, owner, rows):
            return pl.ds(pl.multiple_of(first + owner * rows, 8), rows)

        def scatter(axis, first, rows, owners, source, target, send, recv):
            def copy(step, peer, owner, slot):
                return pltpu.make_async_remote_copy(
                    src_ref=source.at[span(first, owner, rows)],
                    dst_ref=target.at[slot],
                    send_sem=send.at[step], recv_sem=recv.at[slot],
                    device_id={axis: peer}, device_id_type=pl.DeviceIdType.MESH)

            def start():
                me = place[axis]
                each_peer(axis, lambda step, peer, owner: copy(step, peer, owner, me).start(), owners)

                def keep(owner):
                    target[me] = source[span(first, owner, rows), :]

                if_owner(axis, owners, keep)
                unsent.append(lambda: each_peer(
                    axis, lambda step, peer, owner: copy(step, peer, owner, me).wait_send(), owners))

            def wait():
                each_peer(axis, lambda step, peer, owner: copy(step, peer, 0, peer).wait_recv())

            return start, wait

        def gather(axis, first, rows, owners, whole, send, recv):
            def copy(step, peer, owner):
                at = whole.at[span(first, owner, rows)]
                return pltpu.make_async_remote_copy(
                    src_ref=at, dst_ref=at,
                    send_sem=send.at[step], recv_sem=recv.at[owner],
                    device_id={axis: peer}, device_id_type=pl.DeviceIdType.MESH)

            def start(value):
                def share(mine):
                    whole[span(first, mine, rows), :] = value(mine)
                    each_peer(axis, lambda step, peer, owner: copy(step, peer, mine).start())

                if_owner(axis, owners, share)
                unsent.append(lambda: if_owner(axis, owners, lambda mine: each_peer(
                    axis, lambda step, peer, owner: copy(step, peer, mine).wait_send())))

            def wait():
                each_peer(axis, lambda step, peer, owner: copy(step, peer, owner).wait_recv(), owners)

            return start, wait

        for top in range(0, filt, PANEL):
            here = slice(top, top + PANEL)
            angle = dot_nt(filters_ref[here, :], patches_ref[...]) + phases_ref[here, :]
            turns = jnp.floor(angle * (0.5 / math.pi) + 0.5)
            angle = (angle - turns * TURN_HIGH) - turns * TURN_LOW
            square = angle * angle
            value = jnp.full_like(square, COEFFICIENTS[-1])
            for coefficient in COEFFICIENTS[-2::-1]:
                value = value * square + coefficient
            inside = lax.broadcasted_iota(jnp.int32, value.shape, 1) < pos
            feat[here, :] = jnp.where(inside, value, 0.0).astype(jnp.bfloat16)

        def spot_of(row, col):
            return slice((row * (row + 1) // 2 + col) * TILE, (row * (row + 1) // 2 + col + 1) * TILE)

        for top in range(0, filt, PANEL):
            block = dot_nt(feat[top:top + PANEL, :], feat[:top + PANEL, :])
            for row in range(top // TILE, (top + PANEL) // TILE):
                for col in range(row + 1):
                    gram[spot_of(row, col), :] = block[
                        row * TILE - top:(row + 1) * TILE - top, col * TILE:(col + 1) * TILE]

        pl.semaphore_wait(barrier, n_img - 1 + n_blk - 1)

        number, side = place["img"] // 2, lax.rem(place["img"], 2)
        other = place["img"] + 1 - 2 * side

        def to_device(source, target, send, recv, device):
            return pltpu.make_async_remote_copy(
                src_ref=source, dst_ref=target, send_sem=send, recv_sem=recv,
                device_id={"img": device}, device_id_type=pl.DeviceIdType.MESH)

        def each_pair(body):
            for step in range(1, pairs):
                peer = lax.rem(number + step, pairs)
                body(step, peer, 2 * peer + side)

        def gram_chunk(which):
            return gram_all.at[span(side * half, which, rows_gram)]

        def halves(from_side):
            return to_device(gram.at[span(0, from_side, half)], gram_half, gram_s.at[0], gram_r.at[0], other)

        def to_owner(step, peer, slot, device):
            return to_device(gram_sum.at[span(0, peer, rows_gram)], gram_in.at[slot],
                             gram_s.at[step], gram_r.at[1 + slot], device)

        def to_all(step, chunk, device):
            return to_device(gram_chunk(chunk), gram_chunk(chunk), gram_all_s.at[step], gram_all_r.at[chunk], device)

        def to_other(chunk, at_side):
            at = gram_all.at[span(at_side * half, chunk, rows_gram)]
            return to_device(at, at, gram_all_s.at[pairs + chunk], gram_all_r.at[pairs + chunk], other)

        halves(1 - side).start()

        def transfers(axis, turn, g, source, target, whole, sems):
            first, rows = groups[g]
            chunk = chunks[axis]
            at = (turn, g)
            return (scatter(axis, first, chunk, rows // chunk, source.at[turn], target.at[at],
                            sems[0].at[at], sems[1].at[at])
                    + gather(axis, first, chunk, rows // chunk, whole.at[turn],
                             sems[2].at[at], sems[3].at[at]))

        def predict_transfers(turn, g):
            return transfers("blk", turn, g, part, part_in, part_all,
                             (part_s, part_r, part_all_s, part_all_r))

        def project_transfers(step, g):
            return transfers("img", step, g, proj, proj_in, w_all, (proj_s, proj_r, w_s, w_r))

        def rows_of(g):
            first, rows = groups[g]
            return slice(first, first + rows)

        def begin_predict(turn, g, weight_now):
            value = shrink * dot(weight_now.astype(jnp.bfloat16), feat[...])
            part[turn, rows_of(g), :] = value.astype(jnp.bfloat16)
            predict_transfers(turn, g)[0]()

        def middle_predict(turn, g):
            _, wait, share, _ = predict_transfers(turn, g)
            if_owner("blk", groups[g][1] // chunks["blk"], lambda mine: wait())
            share(lambda mine: jnp.sum(part_in[turn, g].astype(jnp.float32), axis=0).astype(jnp.bfloat16))

        def end_predict(turn, g):
            predict_transfers(turn, g)[3]()
            first, rows = groups[g]
            classes = lax.broadcasted_iota(jnp.int32, (rows, pos_pad), 0) + first
            targets = jnp.where(labels_ref[...] == classes, 1.0, 0.0)
            residual = targets - part_all[turn, rows_of(g), :].astype(jnp.float32)
            if turn < ITERS:
                proj[turn, rows_of(g), :] = dot_nt(residual.astype(jnp.bfloat16), feat[...])
                project_transfers(turn, g)[0]()
            else:
                end = min(first + rows, LABELS)
                out_residual[first:end, :] = residual[:end - first, :pos]

        def solve(step, g):
            _, wait, share, _ = project_transfers(step, g)

            def weight_next(mine):
                here = span(groups[g][0], mine, chunks["img"])
                before = weights_ref[here, :] if step == 0 else w_all[step - 1, here, :]
                total = jnp.sum(proj_in[step, g], axis=0)
                p_high = total.astype(jnp.bfloat16)
                high = p_high.astype(jnp.float32)
                both = jnp.concatenate([high, total - high], 0).astype(jnp.bfloat16)
                change = dot(both, x_high[...])
                rows = total.shape[0]
                change = change[:rows] + (change[rows:] + dot(p_high, x_low[...]))
                return before + DAMPING * (expand * change)

            if_owner("img", groups[g][1] // chunks["img"], lambda mine: wait())
            share(weight_next)

        def use_weights(step, g):
            project_transfers(step, g)[3]()
            begin_predict(step + 1, g, w_all[step, rows_of(g), :])
            if step == ITERS - 1:
                first, rows = groups[g]
                end = min(first + rows, LABELS)
                out_weights[first:end, :] = w_all[step, first:end, :]

        every = range(len(groups))
        part[0] = (shrink * dot(weights_ref[...].astype(jnp.bfloat16), feat[...])).astype(jnp.bfloat16)
        halves(side).wait_recv()
        gram_sum[...] = gram[span(0, side, half), :] + gram_half[...]
        each_pair(lambda step, peer, device: to_owner(step, peer, number, device).start())
        gram_in[number] = gram_sum[span(0, number, rows_gram), :]
        for g in every:
            predict_transfers(0, g)[0]()
        each_pair(lambda step, peer, device: to_owner(step, peer, peer, device).wait_recv())
        gram_chunk(number)[...] = jnp.sum(gram_in[...], axis=0)
        each_pair(lambda step, peer, device: to_all(step, number, device).start())
        to_other(number, side).start()
        for g in every:
            middle_predict(0, g)

        def pass_on(step, peer, device):
            to_all(step, peer, device).wait_recv()
            to_other(peer, side).start()

        each_pair(pass_on)
        for chunk in range(pairs):
            to_other(chunk, 1 - side).wait_recv()

        diagonal = (lax.broadcasted_iota(jnp.int32, (TILE, TILE), 0)
                    == lax.broadcasted_iota(jnp.int32, (TILE, TILE), 1))
        scale = scales[0]
        for row in range(tiles):
            for col in range(row + 1):
                block = gram_all[spot_of(row, col), :]
                if row == col:
                    block = block + jnp.where(diagonal, RIDGE * pixels, 0.0)
                start = block * (-scale * scale / upper / upper)
                if row == col:
                    start = start + jnp.where(diagonal, 2.0 * scale / upper, 0.0)
                places = [(row, col, block, start)]
                if row != col:
                    places.append((col, row, block.T, start.T))
                for down, across, h_part, x_part in places:
                    at = (slice(down * TILE, (down + 1) * TILE), slice(across * TILE, (across + 1) * TILE))
                    h_high[at], h_low[at] = split(h_part)
                    x_high[at], x_low[at] = split(x_part)

        def newton(step, carry):
            scale = scales_ref[step]
            y = dot_three(h_high[...], h_low[...], x_high[...], x_low[...])
            same = (lax.broadcasted_iota(jnp.int32, y.shape, 0)
                    == lax.broadcasted_iota(jnp.int32, y.shape, 1))
            y_high[...], y_low[...] = split(jnp.where(same, 2.0, 0.0) - scale * y)
            x = dot_three(x_high[...], x_low[...], y_high[...], y_low[...])
            x_high[...], x_low[...] = split(scale * x)
            return carry

        begun = (len(scales) + 1) // 2
        lax.fori_loop(1, begun, newton, 0)
        for g in every:
            predict_transfers(0, g)[3]()
        classes = lax.broadcasted_iota(jnp.int32, (rows_all, pos_pad), 0)
        targets = jnp.where(labels_ref[...] == classes, 1.0, 0.0)
        residual = targets - part_all[0].astype(jnp.float32)
        proj[0] = dot_nt(residual.astype(jnp.bfloat16), feat[...])
        for g in every:
            project_transfers(0, g)[0]()
        lax.fori_loop(begun, len(scales), newton, 0)

        stages = []
        for step in range(ITERS):
            stages += [
                lambda g, step=step: solve(step, g),
                lambda g, step=step: use_weights(step, g),
                lambda g, step=step: middle_predict(step + 1, g),
                lambda g, step=step: end_predict(step + 1, g),
            ]
        for tick in range(len(stages) + len(groups) - 1):
            for g in every:
                if 0 <= tick - g < len(stages):
                    stages[tick - g](g)
        for wait_sent in unsent:
            wait_sent()
        halves(1 - side).wait_send()
        each_pair(lambda step, peer, device: to_owner(step, peer, number, device).wait_send())
        each_pair(lambda step, peer, device: to_all(step, number, device).wait_send())
        for chunk in range(pairs):
            to_other(chunk, side).wait_send()

    f32, bf16 = jnp.float32, jnp.bfloat16
    square = (filt, filt)
    dma = pltpu.SemaphoreType.DMA
    turns, count = ITERS + 1, len(groups)
    scratch = [
        pltpu.VMEM((filt, pos_pad), bf16),
        pltpu.VMEM((packed, TILE), f32),
        pltpu.VMEM((half, TILE), f32),
        pltpu.VMEM((half, TILE), f32),
        pltpu.VMEM((pairs, rows_gram, TILE), f32),
        pltpu.VMEM((packed, TILE), f32),
        pltpu.VMEM(square, bf16), pltpu.VMEM(square, bf16),
        pltpu.VMEM(square, bf16), pltpu.VMEM(square, bf16),
        pltpu.VMEM(square, bf16), pltpu.VMEM(square, bf16),
        pltpu.VMEM((turns, rows_all, pos_pad), bf16),
        pltpu.VMEM((turns, count, n_blk, chunks["blk"], pos_pad), bf16),
        pltpu.VMEM((turns, rows_all, pos_pad), bf16),
        pltpu.VMEM((ITERS, rows_all, filt), f32),
        pltpu.VMEM((ITERS, count, n_img, chunks["img"], filt), f32),
        pltpu.VMEM((ITERS, rows_all, filt), f32),
        dma((n_img,)), dma((n_img,)), dma((n_img,)), dma((n_img,)),
    ]
    scratch += [dma((turns, count, n_blk))] * 4 + [dma((ITERS, count, n_img))] * 4
    return kernel, scratch, scales, rows_all


def round_up(value, unit):
    return -(-value // unit) * unit


def make_patches(images, pos_pad):
    count = images.shape[0]
    half = SIDE // 2
    pairs = images.reshape(count, SIDE, half, 2 * CHAN)
    pairs = jnp.pad(pairs, ((0, 0), (1, 1), (1, 0), (0, 0)))
    parts = []
    for row in range(3):
        lines = pairs[:, row:row + SIDE:2]
        parts += [lines[:, :, :half], lines[:, :, 1:]]
    patches = jnp.concatenate(parts, axis=-1).reshape(count * half * half, 12 * CHAN)
    return jnp.pad(patches, ((0, pos_pad - patches.shape[0]), (0, 0)))


def solution(mesh):
    n_img, n_blk = mesh.shape["img"], mesh.shape["blk"]

    def shards(images, filters, phases, labels, weights):
        filt, pos = filters.shape[0], labels.shape[0]
        pos_pad = round_up(pos, TILE)
        groups, chunks = make_groups(n_img, n_blk)
        kernel, scratch, scales, rows_all = make_kernel(
            n_img, n_blk, filt, pos, pos_pad, pos * n_img, groups, chunks)
        patches = make_patches(images, pos_pad)
        taps = jnp.pad(filters.reshape(filt, 3, 3 * CHAN), ((0, 0), (0, 0), (CHAN, 0)))
        vmem = pl.BlockSpec(memory_space=pltpu.VMEM)
        return pl.pallas_call(
            kernel,
            out_shape=(jax.ShapeDtypeStruct((LABELS, filt), jnp.float32),
                       jax.ShapeDtypeStruct((LABELS, pos), jnp.float32)),
            in_specs=[vmem] * 5 + [pl.BlockSpec(memory_space=pltpu.SMEM)],
            out_specs=(vmem, vmem),
            scratch_shapes=scratch,
            compiler_params=pltpu.CompilerParams(
                collective_id=0, has_side_effects=True, vmem_limit_bytes=48 * 2**20),
        )(
            patches,
            taps.reshape(filt, 12 * CHAN),
            phases[:, None],
            jnp.pad(labels[None, :], ((0, 0), (0, pos_pad - pos)), constant_values=-1),
            jnp.pad(weights, ((0, rows_all - LABELS), (0, 0))),
            jnp.asarray(np.array(scales, np.float32)),
        )

    return jax.shard_map(
        shards,
        mesh=mesh,
        in_specs=(P("img", None, None), P("blk", None), P("blk"), P("img"), P(None, "blk")),
        out_specs=(P(None, "blk"), P(None, "img")),
        check_vma=False,
    )
```

```python
import math

import jax
import jax.numpy as jnp
import numpy as np
from jax import lax
from jax.experimental import pallas as pl
from jax.experimental.pallas import tpu as pltpu
from jax.sharding import PartitionSpec as P

SIDE = 28
CHAN = 64
LABELS = 150
ITERS = 2
RIDGE = 0.5
DAMPING = 0.75
TILE = 128
PANEL = 256


def cosine_coefficients(degree=6):
    nodes = np.cos((np.arange(400) + 0.5) * np.pi / 400)
    square = (nodes + 1.0) * (np.pi**2 * 1.0005) / 2
    fit = np.polynomial.chebyshev.Chebyshev.fit(square, np.sqrt(2.0) * np.cos(np.sqrt(square)), degree)
    return [float(c) for c in fit.convert(kind=np.polynomial.Polynomial).coef]


COEFFICIENTS = cosine_coefficients()
TURN_HIGH = 6.28125
TURN_LOW = 2.0 * math.pi - TURN_HIGH


def inverse_scales(lowest):
    scales = []
    while 1.0 - lowest > 1e-4:
        scale = 2.0 / (1.0 + lowest)
        scales.append(scale)
        lowest = scale * lowest * (2.0 - scale * lowest)
    return scales


def split(value):
    high = value.astype(jnp.bfloat16)
    return high, (value - high.astype(jnp.float32)).astype(jnp.bfloat16)


def dot(a, b):
    return jnp.dot(a, b, preferred_element_type=jnp.float32)


def dot_nt(a, b):
    return lax.dot_general(a, b, (((1,), (1,)), ((), ())), preferred_element_type=jnp.float32)


def dot_three(a_high, a_low, b_high, b_low):
    return dot(jnp.concatenate([a_high, a_high, a_low], 1), jnp.concatenate([b_high, b_low, b_high], 0))


def make_groups(n_img, n_blk):
    unit = math.lcm(8 * n_img, 16 * n_blk)
    chunks = {"img": unit // n_img, "blk": unit // n_blk}
    last = math.lcm(*chunks.values())
    groups = []
    first = 0
    while first < LABELS:
        rows = min(unit, round_up(LABELS - first, last))
        groups.append((first, rows))
        first += rows
    return groups, chunks


def make_kernel(n_img, n_blk, filt, pos, pos_pad, pixels, groups, chunks):
    features_all = filt * n_blk
    shrink = 1.0 / math.sqrt(features_all)
    expand = math.sqrt(features_all)
    tiles = filt // TILE
    packed = tiles * (tiles + 1) // 2 * TILE
    half = packed // 2
    rows_gram = packed // n_img
    pairs = n_img // 2
    rows_all = sum(rows for _, rows in groups)
    upper = (RIDGE + 2.0 * filt) * pixels
    scales = inverse_scales(RIDGE * pixels / upper)

    def kernel(
        patches_ref, filters_ref, phases_ref, labels_ref, weights_ref, scales_ref,
        out_weights, out_residual,
        feat, gram, gram_half, gram_sum, gram_in, gram_all, h_high, h_low, x_high, x_low, y_high, y_low,
        part, part_in, part_all, proj, proj_in, w_all,
        gram_s, gram_r, gram_all_s, gram_all_r,
        part_s, part_r, part_all_s, part_all_r,
        proj_s, proj_r, w_s, w_r,
    ):
        place = {"img": lax.axis_index("img"), "blk": lax.axis_index("blk")}
        size = {"img": n_img, "blk": n_blk}
        barrier = pltpu.get_barrier_semaphore()

        def each_peer(axis, body, owners=None):
            me, n = place[axis], size[axis]
            stride = 1 if owners is None else n // owners

            def one(step, carry):
                peer = lax.rem(me + step, n)
                if owners is None or owners == n:
                    body(step, peer, peer)
                else:
                    @pl.when((lax.rem(peer, stride) == 0) & (peer < stride * owners))
                    def _():
                        body(step, peer, peer // stride)
                return carry

            if n <= 8:
                for step in range(1, n):
                    one(step, 0)
            else:
                lax.fori_loop(1, n, one, 0)

        def if_owner(axis, owners, body):
            me, n = place[axis], size[axis]
            stride = n // owners
            if owners == n:
                body(me)
            else:
                @pl.when((lax.rem(me, stride) == 0) & (me < stride * owners))
                def _():
                    body(me // stride)

        for axis in size:
            each_peer(axis, lambda step, peer, owner: pl.semaphore_signal(
                barrier, inc=1, device_id={axis: peer}, device_id_type=pl.DeviceIdType.MESH))

        unsent = []

        def span(first, owner, rows):
            return pl.ds(pl.multiple_of(first + owner * rows, 8), rows)

        def scatter(axis, first, rows, owners, source, target, send, recv):
            def copy(step, peer, owner, slot):
                return pltpu.make_async_remote_copy(
                    src_ref=source.at[span(first, owner, rows)],
                    dst_ref=target.at[slot],
                    send_sem=send.at[step], recv_sem=recv.at[slot],
                    device_id={axis: peer}, device_id_type=pl.DeviceIdType.MESH)

            def start():
                me = place[axis]
                each_peer(axis, lambda step, peer, owner: copy(step, peer, owner, me).start(), owners)

                def keep(owner):
                    target[me] = source[span(first, owner, rows), :]

                if_owner(axis, owners, keep)
                unsent.append(lambda: each_peer(
                    axis, lambda step, peer, owner: copy(step, peer, owner, me).wait_send(), owners))

            def wait():
                each_peer(axis, lambda step, peer, owner: copy(step, peer, 0, peer).wait_recv())

            return start, wait

        def gather(axis, first, rows, owners, whole, send, recv):
            def copy(step, peer, owner):
                at = whole.at[span(first, owner, rows)]
                return pltpu.make_async_remote_copy(
                    src_ref=at, dst_ref=at,
                    send_sem=send.at[step], recv_sem=recv.at[owner],
                    device_id={axis: peer}, device_id_type=pl.DeviceIdType.MESH)

            def start(value):
                def share(mine):
                    whole[span(first, mine, rows), :] = value(mine)
                    each_peer(axis, lambda step, peer, owner: copy(step, peer, mine).start())

                if_owner(axis, owners, share)
                unsent.append(lambda: if_owner(axis, owners, lambda mine: each_peer(
                    axis, lambda step, peer, owner: copy(step, peer, mine).wait_send())))

            def wait():
                each_peer(axis, lambda step, peer, owner: copy(step, peer, owner).wait_recv(), owners)

            return start, wait

        for top in range(0, filt, PANEL):
            here = slice(top, top + PANEL)
            angle = dot_nt(filters_ref[here, :], patches_ref[...]) + phases_ref[here, :]
            turns = jnp.floor(angle * (0.5 / math.pi) + 0.5)
            angle = (angle - turns * TURN_HIGH) - turns * TURN_LOW
            square = angle * angle
            value = jnp.full_like(square, COEFFICIENTS[-1])
            for coefficient in COEFFICIENTS[-2::-1]:
                value = value * square + coefficient
            inside = lax.broadcasted_iota(jnp.int32, value.shape, 1) < pos
            feat[here, :] = jnp.where(inside, value, 0.0).astype(jnp.bfloat16)

        def spot_of(row, col):
            return slice((row * (row + 1) // 2 + col) * TILE, (row * (row + 1) // 2 + col + 1) * TILE)

        for top in range(0, filt, PANEL):
            block = dot_nt(feat[top:top + PANEL, :], feat[:top + PANEL, :])
            for row in range(top // TILE, (top + PANEL) // TILE):
                for col in range(row + 1):
                    gram[spot_of(row, col), :] = block[
                        row * TILE - top:(row + 1) * TILE - top, col * TILE:(col + 1) * TILE]

        pl.semaphore_wait(barrier, n_img - 1 + n_blk - 1)

        number, side = place["img"] // 2, lax.rem(place["img"], 2)
        other = place["img"] + 1 - 2 * side

        def to_device(source, target, send, recv, device):
            return pltpu.make_async_remote_copy(
                src_ref=source, dst_ref=target, send_sem=send, recv_sem=recv,
                device_id={"img": device}, device_id_type=pl.DeviceIdType.MESH)

        def each_pair(body):
            for step in range(1, pairs):
                peer = lax.rem(number + step, pairs)
                body(step, peer, 2 * peer + side)

        def gram_chunk(which):
            return gram_all.at[span(side * half, which, rows_gram)]

        def halves(from_side):
            return to_device(gram.at[span(0, from_side, half)], gram_half, gram_s.at[0], gram_r.at[0], other)

        def to_owner(step, peer, slot, device):
            return to_device(gram_sum.at[span(0, peer, rows_gram)], gram_in.at[slot],
                             gram_s.at[step], gram_r.at[1 + slot], device)

        def to_all(step, chunk, device):
            return to_device(gram_chunk(chunk), gram_chunk(chunk), gram_all_s.at[step], gram_all_r.at[chunk], device)

        def to_other(chunk, at_side):
            at = gram_all.at[span(at_side * half, chunk, rows_gram)]
            return to_device(at, at, gram_all_s.at[pairs + chunk], gram_all_r.at[pairs + chunk], other)

        halves(1 - side).start()

        def transfers(axis, turn, g, source, target, whole, sems):
            first, rows = groups[g]
            chunk = chunks[axis]
            at = (turn, g)
            return (scatter(axis, first, chunk, rows // chunk, source.at[turn], target.at[at],
                            sems[0].at[at], sems[1].at[at])
                    + gather(axis, first, chunk, rows // chunk, whole.at[turn],
                             sems[2].at[at], sems[3].at[at]))

        def predict_transfers(turn, g):
            return transfers("blk", turn, g, part, part_in, part_all,
                             (part_s, part_r, part_all_s, part_all_r))

        def project_transfers(step, g):
            return transfers("img", step, g, proj, proj_in, w_all, (proj_s, proj_r, w_s, w_r))

        def rows_of(g):
            first, rows = groups[g]
            return slice(first, first + rows)

        def begin_predict(turn, g, weight_now):
            value = shrink * dot(weight_now.astype(jnp.bfloat16), feat[...])
            part[turn, rows_of(g), :] = value.astype(jnp.bfloat16)
            predict_transfers(turn, g)[0]()

        def middle_predict(turn, g):
            _, wait, share, _ = predict_transfers(turn, g)
            if_owner("blk", groups[g][1] // chunks["blk"], lambda mine: wait())
            share(lambda mine: jnp.sum(part_in[turn, g].astype(jnp.float32), axis=0).astype(jnp.bfloat16))

        def end_predict(turn, g):
            predict_transfers(turn, g)[3]()
            first, rows = groups[g]
            classes = lax.broadcasted_iota(jnp.int32, (rows, pos_pad), 0) + first
            targets = jnp.where(labels_ref[...] == classes, 1.0, 0.0)
            residual = targets - part_all[turn, rows_of(g), :].astype(jnp.float32)
            if turn < ITERS:
                proj[turn, rows_of(g), :] = dot_nt(residual.astype(jnp.bfloat16), feat[...])
                project_transfers(turn, g)[0]()
            else:
                end = min(first + rows, LABELS)
                out_residual[first:end, :] = residual[:end - first, :pos]

        def solve(step, g):
            _, wait, share, _ = project_transfers(step, g)

            def weight_next(mine):
                here = span(groups[g][0], mine, chunks["img"])
                before = weights_ref[here, :] if step == 0 else w_all[step - 1, here, :]
                total = jnp.sum(proj_in[step, g], axis=0)
                p_high = total.astype(jnp.bfloat16)
                high = p_high.astype(jnp.float32)
                both = jnp.concatenate([high, total - high], 0).astype(jnp.bfloat16)
                change = dot(both, x_high[...])
                rows = total.shape[0]
                change = change[:rows] + (change[rows:] + dot(p_high, x_low[...]))
                return before + DAMPING * (expand * change)

            if_owner("img", groups[g][1] // chunks["img"], lambda mine: wait())
            share(weight_next)

        def use_weights(step, g):
            project_transfers(step, g)[3]()
            begin_predict(step + 1, g, w_all[step, rows_of(g), :])
            if step == ITERS - 1:
                first, rows = groups[g]
                end = min(first + rows, LABELS)
                out_weights[first:end, :] = w_all[step, first:end, :]

        every = range(len(groups))
        part[0] = (shrink * dot(weights_ref[...].astype(jnp.bfloat16), feat[...])).astype(jnp.bfloat16)
        halves(side).wait_recv()
        gram_sum[...] = gram[span(0, side, half), :] + gram_half[...]
        each_pair(lambda step, peer, device: to_owner(step, peer, number, device).start())
        gram_in[number] = gram_sum[span(0, number, rows_gram), :]
        for g in every:
            predict_transfers(0, g)[0]()
        each_pair(lambda step, peer, device: to_owner(step, peer, peer, device).wait_recv())
        gram_chunk(number)[...] = jnp.sum(gram_in[...], axis=0)
        each_pair(lambda step, peer, device: to_all(step, number, device).start())
        to_other(number, side).start()
        for g in every:
            middle_predict(0, g)

        def pass_on(step, peer, device):
            to_all(step, peer, device).wait_recv()
            to_other(peer, side).start()

        each_pair(pass_on)
        for chunk in range(pairs):
            to_other(chunk, 1 - side).wait_recv()

        diagonal = (lax.broadcasted_iota(jnp.int32, (TILE, TILE), 0)
                    == lax.broadcasted_iota(jnp.int32, (TILE, TILE), 1))
        scale = scales[0]
        for row in range(tiles):
            for col in range(row + 1):
                block = gram_all[spot_of(row, col), :]
                if row == col:
                    block = block + jnp.where(diagonal, RIDGE * pixels, 0.0)
                start = block * (-scale * scale / upper / upper)
                if row == col:
                    start = start + jnp.where(diagonal, 2.0 * scale / upper, 0.0)
                places = [(row, col, block, start)]
                if row != col:
                    places.append((col, row, block.T, start.T))
                for down, across, h_part, x_part in places:
                    at = (slice(down * TILE, (down + 1) * TILE), slice(across * TILE, (across + 1) * TILE))
                    h_high[at], h_low[at] = split(h_part)
                    x_high[at], x_low[at] = split(x_part)

        def newton(step, carry):
            scale = scales_ref[step]
            y = dot_three(h_high[...], h_low[...], x_high[...], x_low[...])
            same = (lax.broadcasted_iota(jnp.int32, y.shape, 0)
                    == lax.broadcasted_iota(jnp.int32, y.shape, 1))
            y_high[...], y_low[...] = split(jnp.where(same, 2.0, 0.0) - scale * y)
            x = dot_three(x_high[...], x_low[...], y_high[...], y_low[...])
            x_high[...], x_low[...] = split(scale * x)
            return carry

        begun = (len(scales) + 1) // 2
        lax.fori_loop(1, begun, newton, 0)
        for g in every:
            predict_transfers(0, g)[3]()
        classes = lax.broadcasted_iota(jnp.int32, (rows_all, pos_pad), 0)
        targets = jnp.where(labels_ref[...] == classes, 1.0, 0.0)
        residual = targets - part_all[0].astype(jnp.float32)
        proj[0] = dot_nt(residual.astype(jnp.bfloat16), feat[...])
        for g in every:
            project_transfers(0, g)[0]()
        lax.fori_loop(begun, len(scales), newton, 0)

        stages = []
        for step in range(ITERS):
            stages += [
                lambda g, step=step: solve(step, g),
                lambda g, step=step: use_weights(step, g),
                lambda g, step=step: middle_predict(step + 1, g),
                lambda g, step=step: end_predict(step + 1, g),
            ]
        for tick in range(len(stages) + len(groups) - 1):
            for g in every:
                if 0 <= tick - g < len(stages):
                    stages[tick - g](g)
        for wait_sent in unsent:
            wait_sent()
        halves(1 - side).wait_send()
        each_pair(lambda step, peer, device: to_owner(step, peer, number, device).wait_send())
        each_pair(lambda step, peer, device: to_all(step, number, device).wait_send())
        for chunk in range(pairs):
            to_other(chunk, side).wait_send()

    f32, bf16 = jnp.float32, jnp.bfloat16
    square = (filt, filt)
    dma = pltpu.SemaphoreType.DMA
    turns, count = ITERS + 1, len(groups)
    scratch = [
        pltpu.VMEM((filt, pos_pad), bf16),
        pltpu.VMEM((packed, TILE), f32),
        pltpu.VMEM((half, TILE), f32),
        pltpu.VMEM((half, TILE), f32),
        pltpu.VMEM((pairs, rows_gram, TILE), f32),
        pltpu.VMEM((packed, TILE), f32),
        pltpu.VMEM(square, bf16), pltpu.VMEM(square, bf16),
        pltpu.VMEM(square, bf16), pltpu.VMEM(square, bf16),
        pltpu.VMEM(square, bf16), pltpu.VMEM(square, bf16),
        pltpu.VMEM((turns, rows_all, pos_pad), bf16),
        pltpu.VMEM((turns, count, n_blk, chunks["blk"], pos_pad), bf16),
        pltpu.VMEM((turns, rows_all, pos_pad), bf16),
        pltpu.VMEM((ITERS, rows_all, filt), f32),
        pltpu.VMEM((ITERS, count, n_img, chunks["img"], filt), f32),
        pltpu.VMEM((ITERS, rows_all, filt), f32),
        dma((n_img,)), dma((n_img,)), dma((n_img,)), dma((n_img,)),
    ]
    scratch += [dma((turns, count, n_blk))] * 4 + [dma((ITERS, count, n_img))] * 4
    return kernel, scratch, scales, rows_all


def round_up(value, unit):
    return -(-value // unit) * unit


def make_patches(images, pos_pad):
    count = images.shape[0]
    half = SIDE // 2
    pairs = images.reshape(count, SIDE, half, 2 * CHAN)
    pairs = jnp.pad(pairs, ((0, 0), (1, 1), (1, 0), (0, 0)))
    parts = []
    for row in range(3):
        lines = pairs[:, row:row + SIDE:2]
        parts += [lines[:, :, :half], lines[:, :, 1:]]
    patches = jnp.concatenate(parts, axis=-1).reshape(count * half * half, 12 * CHAN)
    return jnp.pad(patches, ((0, pos_pad - patches.shape[0]), (0, 0)))


def solution(mesh):
    n_img, n_blk = mesh.shape["img"], mesh.shape["blk"]

    def shards(images, filters, phases, labels, weights):
        filt, pos = filters.shape[0], labels.shape[0]
        pos_pad = round_up(pos, TILE)
        groups, chunks = make_groups(n_img, n_blk)
        kernel, scratch, scales, rows_all = make_kernel(
            n_img, n_blk, filt, pos, pos_pad, pos * n_img, groups, chunks)
        patches = make_patches(images, pos_pad)
        taps = jnp.pad(filters.reshape(filt, 3, 3 * CHAN), ((0, 0), (0, 0), (CHAN, 0)))
        vmem = pl.BlockSpec(memory_space=pltpu.VMEM)
        return pl.pallas_call(
            kernel,
            out_shape=(jax.ShapeDtypeStruct((LABELS, filt), jnp.float32),
                       jax.ShapeDtypeStruct((LABELS, pos), jnp.float32)),
            in_specs=[vmem] * 5 + [pl.BlockSpec(memory_space=pltpu.SMEM)],
            out_specs=(vmem, vmem),
            scratch_shapes=scratch,
            compiler_params=pltpu.CompilerParams(
                collective_id=0, has_side_effects=True, vmem_limit_bytes=48 * 2**20),
        )(
            patches,
            taps.reshape(filt, 12 * CHAN),
            phases[:, None],
            jnp.pad(labels[None, :], ((0, 0), (0, pos_pad - pos)), constant_values=-1),
            jnp.pad(weights, ((0, rows_all - LABELS), (0, 0))),
            jnp.asarray(np.array(scales, np.float32)),
        )

    return jax.shard_map(
        shards,
        mesh=mesh,
        in_specs=(P("img", None, None), P("blk", None), P("blk"), P("img"), P(None, "blk")),
        out_specs=(P(None, "blk"), P(None, "img")),
        check_vma=False,
    )
```
